32 devices in a mesh: row: 4 (over y, x), col: 8 (over z, core).
Axes of the slice: x: 2, y: 2, z: 4, core: 2. Of those that a mesh axis runs over, the one named last changes fastest.
Arguments:
- ancestor: float32 [2, 1024, 1024], P(None, 'row', 'col')
- panel: float32 [2, 1024, 512], P(None, 'col'), may hold values from -0.75 to 0.75
- factor_inv: float32 [2, 512, 512], P(None, 'row'), as said below
- pattern: int32 [2, 4], replicated, may hold values from 0 to 3, each once within a row
Outputs:
- column_block: float32 [2, 1024, 512], P(None, ('row', 'col'))
- diagonal_inv: float32 [2, 512], replicated
The draws below stay inside these ranges and needn't reach their ends.
Inputs may be any that keep to these rules, and one draw needn't show every extreme that they name: `pattern`: each row names each of the 4 tile positions exactly once. `factor_inv`: each block is lower triangular with its diagonal between 0.5 and 2.
All inputs are finite; a program needn't handle non-finite values.
Results may differ from the reference program's by a relative error of at most 0.0001.
Values sent between devices are 32-bit elements; how exact they have to be, the bound alone decides.
No kernel may reach another device: no remote copies, remote signals or barrier semaphores. Data moves between devices by JAX's collectives and lax.ppermute only.
A program may use at most 64 MiB of HBM per device.

```python
import math
import jax
import jax.numpy as jnp
from jax import lax

B = 256
W = 512
S = 2
R = 4
RB = 1024


def draw_ancestor(key, part):
    key = jax.random.fold_in(key, 11)
    first_key, second_key = jax.random.split(key)
    noise = jax.random.normal(first_key, (S, RB, RB), jnp.float32)
    offdiag = (noise + jnp.swapaxes(noise, 1, 2)) * (0.5 / math.sqrt(RB))
    levels = jnp.exp(jax.random.uniform(second_key, (S, RB), jnp.float32, math.log(0.5), math.log(2.0)))
    rows_idx = jnp.arange(RB, dtype=jnp.int32)
    on_diag = rows_idx[:, None] == rows_idx[None, :]
    return jnp.where(on_diag[None], offdiag + levels[:, :, None], offdiag)


def draw_factor_inv(key, part):
    key = jax.random.fold_in(key, 12)
    first_key, second_key = jax.random.split(key)
    noise = jax.random.normal(first_key, (S, W, W), jnp.float32)
    levels = jnp.exp(jax.random.uniform(second_key, (S, W), jnp.float32, math.log(0.5), math.log(2.0)))
    rows_idx = jnp.arange(W, dtype=jnp.int32)
    below = rows_idx[:, None] > rows_idx[None, :]
    on_diag = rows_idx[:, None] == rows_idx[None, :]
    lower = jnp.where(below[None], noise / math.sqrt(W), 0.0)
    return jnp.where(on_diag[None], levels[:, :, None], lower).astype(jnp.float32)


def block_scale(stream_key, dims, cuts, low, largest):
    level = 1.0
    for dim, parts in cuts:
        heights = jax.random.uniform(jax.random.fold_in(jax.random.fold_in(stream_key, 6), dim), (parts,), jnp.float32, low / len(cuts), largest / len(cuts))
        level = level * jnp.repeat(jnp.exp(heights), dims[dim] // parts).reshape((-1,) + (1,) * (len(dims) - 1 - dim))
    return level


def scatter_about(own_key, shape, width, bound, cuts=(), kind=jnp.bfloat16):
    entries = width * jax.random.normal(own_key, shape, jnp.float32)
    if cuts:
        entries = entries * block_scale(own_key, shape, cuts, -0.22, 0.18)
    return jnp.clip(entries, -bound, bound).astype(kind)


def setup_inputs(seed: int = 0) -> dict:
    seeds = jax.random.split(jax.random.key(seed), 5)
    return {
        "ancestor": draw_ancestor(jax.random.fold_in(seeds[4], 71), 0),
        "panel": scatter_about(seeds[1], (S, RB, W), (B // 4) ** -0.5, 0.75, ((1, 8),), jnp.float32),
        "factor_inv": draw_factor_inv(jax.random.fold_in(seeds[4], 71), 0),
        "pattern": jax.vmap(lambda own: jax.random.permutation(own, R))(jax.random.split(seeds[3], S)).reshape((S, R)).astype(jnp.int32),
    }


def reference(ancestor, panel, factor_inv, pattern):
    highest = lax.Precision.HIGHEST
    scaled_panel = jnp.einsum('srw,swv->srv', panel, factor_inv, precision=highest)
    tiles_view = scaled_panel.reshape(S, R, B, W)
    blocks = jnp.arange(R, dtype=jnp.int32)
    choose = (pattern[:, :, None] == blocks[None, None, :]).astype(jnp.float32)
    spread = jnp.einsum('srn,srbw->snbw', choose, tiles_view, precision=highest).reshape(S, RB, W)
    product = jnp.einsum('sij,sjw->siw', ancestor, spread, precision=highest)
    column_block = -product
    diagonal_inv = jnp.sum(factor_inv * factor_inv, axis=1) + jnp.sum(spread * product, axis=1)
    return column_block, diagonal_inv
```

```python
import jax
import jax.numpy as jnp
from jax import lax
from jax.sharding import PartitionSpec as P

B = 256


def pick_rows(pieces, pattern, first):
    count = pieces.shape[0]
    per_tile = count // pattern.shape[1]
    tile, within = first // per_tile, first % per_tile
    picked = []
    for s in range(pattern.shape[0]):
        stored = jnp.argmax(pattern[s] == tile).astype(jnp.int32)
        chunk = stored * per_tile + within
        picked.append(lax.dynamic_index_in_dim(pieces[:, s], chunk, 0, keepdims=False))
    return jnp.stack(picked)


def solution(mesh):
    rows, cols = mesh.shape["row"], mesh.shape["col"]
    highest = lax.Precision.HIGHEST

    def per_device(ancestor, panel, factor_inv, pattern):
        row = lax.axis_index("row")
        col = lax.axis_index("col")
        depth = factor_inv.shape[1]
        mine = lax.dynamic_slice_in_dim(panel, row * depth, depth, axis=2)
        part = jnp.einsum("srw,swv->srv", mine, factor_inv, precision=highest)
        scaled = lax.psum_scatter(part, "row", scatter_dimension=1, tiled=True)
        pieces = lax.all_gather(scaled, "col", axis=0, tiled=False)
        chosen = pick_rows(pieces, pattern, col)
        swap = [(r * cols + c, c * rows + r) for r in range(rows) for c in range(cols)]
        own_rows = lax.ppermute(chosen, ("row", "col"), swap)
        spread = lax.all_gather(chosen, "row", axis=1, tiled=True)
        partial = jnp.einsum("sij,sjw->siw", ancestor, spread, precision=highest)
        product = lax.psum_scatter(partial, "col", scatter_dimension=1, tiled=True)
        squares = jnp.sum(factor_inv * factor_inv, axis=1)
        terms = jnp.sum(own_rows * product, axis=1) + jnp.where(col == 0, squares, 0.0)
        diagonal_inv = lax.psum(terms, ("row", "col"))
        return -product, diagonal_inv

    in_specs = (P(None, "row", "col"), P(None, "col", None), P(None, "row", None), P())
    out_specs = (P(None, ("row", "col"), None), P())
    return jax.shard_map(
        per_device, mesh=mesh, in_specs=in_specs, out_specs=out_specs, check_vma=False
    )
```

```python
import jax
import jax.numpy as jnp
from jax import lax
from jax.sharding import PartitionSpec as P

B = 256


def solution(mesh):
    rows, cols = mesh.shape["row"], mesh.shape["col"]
    highest = lax.Precision.HIGHEST

    def per_device(ancestor, panel, factor_inv, pattern):
        row = lax.axis_index("row")
        col = lax.axis_index("col")
        groups, chunk, width = panel.shape
        quarter = chunk // rows
        part = width // cols
        out_rows = ancestor.shape[1] // cols

        mine = lax.dynamic_slice_in_dim(panel, row * quarter, quarter, axis=1)
        pieces = lax.all_gather(mine, "col", axis=0)
        wide = lax.all_gather(ancestor, "col", axis=0)
        columns = lax.dynamic_slice_in_dim(factor_inv, col * part, part, axis=2)
        columns = lax.all_gather(columns, "row", axis=1, tiled=True)

        scaled = jnp.einsum("csqw,swk->cqsk", pieces, columns, precision=highest)
        scaled = scaled.reshape(cols, quarter, groups * part)
        scaled = lax.all_gather(scaled, "row", axis=1, tiled=True)
        scaled = scaled.reshape(pattern.shape[1], B, groups, part)
        order = jnp.argsort(pattern, axis=1)
        products, terms = [], []
        for s in range(groups):
            spread = jnp.take(scaled[:, :, s], order[s], axis=0).reshape(-1, part)
            product = jnp.einsum(
                "cij,cjk->ik", wide[:, s], spread.reshape(cols, chunk, part), precision=highest
            )
            own = lax.dynamic_slice_in_dim(spread, row * product.shape[0], product.shape[0], axis=0)
            squares = jnp.where(row == 0, jnp.sum(columns[s] * columns[s], axis=0), 0.0)
            terms.append(jnp.sum(own * product, axis=0) + squares)
            products.append(product)
        product = jnp.concatenate(products, axis=1).reshape(cols, out_rows, groups * part)
        term = jnp.concatenate(terms)
        tail = jnp.broadcast_to(term, (cols, 8, groups * part))
        moved = lax.all_to_all(jnp.concatenate([product, tail], axis=1), "col", 0, 0)
        moved = moved.reshape(cols, out_rows + 8, groups, part)
        moved = moved.transpose(2, 1, 0, 3).reshape(groups, out_rows + 8, width)
        local = moved[:, out_rows]
        total = local
        for shift in range(1, rows):
            total = total + lax.ppermute(
                local, "row", [(r, (r + shift) % rows) for r in range(rows)]
            )
        return -moved[:, :out_rows], total

    in_specs = (P(None, "row", "col"), P(None, "col", None), P(None, "row", None), P())
    out_specs = (P(None, ("row", "col"), None), P())
    return jax.shard_map(
        per_device, mesh=mesh, in_specs=in_specs, out_specs=out_specs, check_vma=False
    )
```

```python
import jax
import jax.numpy as jnp
from jax import lax
from jax.sharding import Mesh, PartitionSpec as P

B = 256


def solution(mesh):
    rows, cols = mesh.shape["row"], mesh.shape["col"]
    cores, deep = 2, cols // 2
    fine = Mesh(mesh.devices.reshape(rows, deep, cores), ("row", "z", "core"))
    highest = lax.Precision.HIGHEST

    def shifted(array, axis, size, shift):
        return lax.ppermute(array, axis, [(i, (i + shift) % size) for i in range(size)])

    def per_device(ancestor, panel, factor_inv, pattern):
        row = lax.axis_index("row")
        z = lax.axis_index("z")
        core = lax.axis_index("core")
        groups, chunk, width = panel.shape
        depth = factor_inv.shape[1]
        part = width // deep
        quarter = B // rows
        out_rows = ancestor.shape[1] // cols

        def of(array, s):
            return lax.dynamic_index_in_dim(array, s, 0, keepdims=False)

        def both(mine, other, axis):
            first = jnp.where(core == 0, mine, other)
            second = jnp.where(core == 0, other, mine)
            return jnp.concatenate([first, second], axis=axis)

        panel = lax.dynamic_slice_in_dim(panel, row * depth, depth, axis=2)
        panel_other = shifted(of(panel, 1 - core), "core", cores, 1)
        ancestor_other = shifted(of(ancestor, 1 - core), "core", cores, 1)
        wide = both(of(ancestor, core), ancestor_other, 1)
        wide = lax.all_gather(wide, "z", axis=0)
        tile = both(of(panel, core), panel_other, 0)
        factor = of(factor_inv, core)

        partial = jnp.dot(tile, factor, precision=highest)

        def rows_of(r):
            return lax.dynamic_slice_in_dim(partial, r * quarter, quarter, axis=0)

        scaled = rows_of(row)
        for shift in range(1, rows):
            scaled = scaled + shifted(rows_of((row + shift) % rows), "row", rows, shift)

        def columns_of(array, c):
            return lax.dynamic_slice_in_dim(array, c * part, part, axis=1)

        slots = [columns_of(scaled, z)]
        for shift in range(1, deep):
            slots.append(shifted(columns_of(scaled, (z + shift) % deep), "z", deep, shift))
        slots = lax.all_gather(jnp.stack(slots), "row", axis=1)

        place = of(pattern, core)
        stored = jnp.arange(deep, dtype=jnp.int32)
        stored = jnp.sum(jnp.where(place[:, None] == stored[None, :], stored[:, None], 0), axis=0)
        spread = jnp.take(slots, (z - stored) % deep, axis=0, mode="clip")
        spread = spread.reshape(deep, B, part)
        product = jnp.einsum("tij,tjk->ik", wide, spread, precision=highest)

        own = lax.dynamic_slice_in_dim(
            spread.reshape(deep * B, part), row * product.shape[0], product.shape[0], axis=0
        )
        term = jnp.sum(own * product, axis=0) + jnp.sum(columns_of(factor, z) ** 2, axis=0)

        tail = jnp.broadcast_to(term, (cols, 8, part))
        sent = jnp.concatenate([product.reshape(cols, out_rows, part), tail], axis=1)
        moved = lax.all_to_all(sent, ("z", "core"), 0, 0)
        moved = moved.reshape(deep, groups, out_rows + 8, part)
        moved = moved.transpose(1, 2, 0, 3).reshape(groups, out_rows + 8, width)
        local = moved[:, out_rows]
        total = local
        for shift in range(1, rows):
            total = total + shifted(local, "row", rows, shift)
        return -moved[:, :out_rows], total

    col = ("z", "core")
    in_specs = (P(None, "row", col), P(None, col, None), P(None, "row", None), P())
    out_specs = (P(None, ("row", "z", "core"), None), P())
    return jax.shard_map(
        per_device, mesh=fine, in_specs=in_specs, out_specs=out_specs, check_vma=False
    )
```

```python
import jax
import jax.numpy as jnp
from jax import lax
from jax.sharding import Mesh, PartitionSpec as P

B = 256


def solution(mesh):
    rows, cols = mesh.shape["row"], mesh.shape["col"]
    cores, deep = 2, cols // 2
    fine = Mesh(mesh.devices.reshape(rows, deep, cores), ("row", "z", "core"))
    highest = lax.Precision.HIGHEST

    def shifted(array, axis, size, shift):
        return lax.ppermute(array, axis, [(i, (i + shift) % size) for i in range(size)])

    def gathered(array, axis, size):
        return [array] + [shifted(array, axis, size, d) for d in range(1, size)]

    def per_device(ancestor, panel, factor_inv, pattern):
        row = lax.axis_index("row")
        z = lax.axis_index("z")
        core = lax.axis_index("core")
        _, chunk, width = panel.shape
        depth = factor_inv.shape[1]
        part = width // deep
        quarter = B // rows
        out_rows = ancestor.shape[1] // cols

        def of(array, s):
            return lax.dynamic_index_in_dim(array, s, 0, keepdims=False)

        def both(mine, other, axis):
            first = jnp.where(core == 0, mine, other)
            second = jnp.where(core == 0, other, mine)
            return jnp.concatenate([first, second], axis=axis)

        panel = lax.dynamic_slice_in_dim(panel, row * depth, depth, axis=2)
        panel_other = shifted(of(panel, 1 - core), "core", cores, 1)
        ancestor_other = shifted(of(ancestor, 1 - core), "core", cores, 1)
        wide = both(of(ancestor, core), ancestor_other, 1)
        wide = jnp.stack(gathered(wide, "z", deep))
        tile = both(of(panel, core), panel_other, 0)
        factor = of(factor_inv, core)

        partial = jnp.dot(tile, factor, precision=highest)

        def rows_of(r):
            return lax.dynamic_slice_in_dim(partial, r * quarter, quarter, axis=0)

        scaled = rows_of(row)
        for shift in range(1, rows):
            scaled = scaled + shifted(rows_of((row + shift) % rows), "row", rows, shift)

        def columns_of(array, c):
            return lax.dynamic_slice_in_dim(array, c * part, part, axis=1)

        slots = [columns_of(scaled, z)]
        for shift in range(1, deep):
            slots.append(shifted(columns_of(scaled, (z + shift) % deep), "z", deep, shift))
        slots = jnp.stack(gathered(jnp.stack(slots), "row", rows))

        place = of(pattern, core)
        stored = jnp.arange(deep, dtype=jnp.int32)
        stored = jnp.sum(jnp.where(place[:, None] == stored[None, :], stored[:, None], 0), axis=0)
        tiles = (z - jnp.arange(deep, dtype=jnp.int32)) % deep
        quarters = (row - jnp.arange(rows, dtype=jnp.int32)) % rows
        from_z = (z - jnp.take(stored, tiles, mode="clip")) % deep
        spread = slots[quarters[None, :], from_z[:, None]].reshape(deep, B, part)
        product = jnp.einsum("tij,tjk->ik", wide, spread, precision=highest)

        held = product.shape[0] // B
        own = jnp.concatenate([of(spread, (z - (row * held + t)) % deep) for t in range(held)])
        term = jnp.sum(own * product, axis=0) + jnp.sum(columns_of(factor, z) ** 2, axis=0)

        tail = jnp.broadcast_to(term, (cores, 8, part))

        def rows_for(c):
            block = lax.dynamic_slice_in_dim(product, c * cores * out_rows, cores * out_rows)
            block = block.reshape(cores, out_rows, part)
            return jnp.concatenate([block, tail], axis=1)

        moved = [rows_for(z)]
        for shift in range(1, deep):
            moved.append(shifted(rows_for((z + shift) % deep), "z", deep, shift))
        order = (z - jnp.arange(deep, dtype=jnp.int32)) % deep
        moved = jnp.take(jnp.stack(moved), order, axis=0, mode="clip")
        moved = moved.transpose(1, 2, 0, 3).reshape(cores, out_rows + 8, width)
        other = shifted(of(moved, 1 - core), "core", cores, 1)
        mine = of(moved, core)
        first = jnp.where(core == 0, mine, other)
        second = jnp.where(core == 0, other, mine)
        moved = jnp.stack([first, second])
        local = moved[:, out_rows]
        total = local
        for shift in range(1, rows):
            total = total + shifted(local, "row", rows, shift)
        return -moved[:, :out_rows], total

    col = ("z", "core")
    in_specs = (P(None, "row", col), P(None, col, None), P(None, "row", None), P())
    out_specs = (P(None, ("row", "z", "core"), None), P())
    return jax.shard_map(
        per_device, mesh=fine, in_specs=in_specs, out_specs=out_specs, check_vma=False
    )
```

```python
import jax
import jax.numpy as jnp
from jax import lax
from jax.sharding import Mesh, PartitionSpec as P

B = 256


def solution(mesh):
    rows, cols = mesh.shape["row"], mesh.shape["col"]
    cores, deep = 2, cols // 2
    fine = Mesh(mesh.devices.reshape(rows, deep, cores), ("row", "z", "core"))
    highest = lax.Precision.HIGHEST

    def shifted(array, axis, size, shift):
        return lax.ppermute(array, axis, [(i, (i + shift) % size) for i in range(size)])

    def gathered(array, axis, size):
        return [array] + [shifted(array, axis, size, d) for d in range(1, size)]

    def per_device(ancestor, panel, factor_inv, pattern):
        row = lax.axis_index("row")
        z = lax.axis_index("z")
        core = lax.axis_index("core")
        _, chunk, width = panel.shape
        depth = factor_inv.shape[1]
        part = width // deep
        piece = chunk // rows
        quarter = cores * piece
        out_rows = ancestor.shape[1] // cols

        def of(array, s):
            return lax.dynamic_index_in_dim(array, s, 0, keepdims=False)

        def swapped(array):
            other = shifted(of(array, 1 - core), "core", cores, 1)
            mine = of(array, core)
            return jnp.stack([jnp.where(core == 0, mine, other), jnp.where(core == 0, other, mine)])

        def after(array, far, shift):
            if shift < deep:
                array, got = lax.optimization_barrier((array, far[shift - 1]))
                far = far[: shift - 1] + [got] + far[shift:]
            return array, far

        far = [shifted(ancestor, "z", deep, d) for d in range(1, deep)]

        mine = lax.dynamic_slice_in_dim(panel, row * depth, depth, axis=2)
        partial = jnp.einsum("srw,swv->srv", mine, factor_inv, precision=highest)

        def rows_of(r):
            return lax.dynamic_slice_in_dim(partial, r * piece, piece, axis=1)

        scaled = rows_of(row)
        for shift in range(1, rows):
            scaled = scaled + shifted(rows_of((row + shift) % rows), "row", rows, shift)
        scaled, far = after(scaled, far, 2)
        scaled = swapped(scaled)

        def columns_of(array, c):
            return lax.dynamic_slice_in_dim(array, c * part, part, axis=1)

        scaled = scaled.reshape(quarter, width)
        slots = [columns_of(scaled, z)]
        for shift in range(1, deep):
            slots.append(shifted(columns_of(scaled, (z + shift) % deep), "z", deep, shift))
        slots, far = after(jnp.stack(slots), far, 1)
        slots = jnp.stack(gathered(slots, "row", rows))
        slots = slots.reshape(rows, deep, cores, piece, part)

        place = of(pattern, core)
        stored = jnp.arange(deep, dtype=jnp.int32)
        stored = jnp.sum(jnp.where(place[:, None] == stored[None, :], stored[:, None], 0), axis=0)
        tiles = (z - jnp.arange(deep, dtype=jnp.int32)) % deep
        quarters = (row - jnp.arange(rows, dtype=jnp.int32)) % rows
        from_z = (z - jnp.take(stored, tiles, mode="clip")) % deep
        spread = slots[quarters[None, :], from_z[:, None]]
        spread = spread.transpose(0, 2, 1, 3, 4).reshape(deep, cores, chunk, part)
        wide = jnp.stack([swapped(a) for a in [ancestor] + far])
        product = jnp.einsum("tcij,tcjk->ik", wide, spread, precision=highest)
        spread = spread.reshape(deep, B, part)

        held = product.shape[0] // B
        own = jnp.concatenate([of(spread, (z - (row * held + t)) % deep) for t in range(held)])
        term = jnp.sum(own * product, axis=0) + jnp.sum(columns_of(of(factor_inv, core), z) ** 2, axis=0)

        tail = jnp.broadcast_to(term, (cores, 8, part))

        def rows_for(c):
            block = lax.dynamic_slice_in_dim(product, c * cores * out_rows, cores * out_rows)
            block = block.reshape(cores, out_rows, part)
            return jnp.concatenate([block, tail], axis=1)

        moved = [rows_for(z)]
        for shift in range(1, deep):
            moved.append(shifted(rows_for((z + shift) % deep), "z", deep, shift))
        order = (z - jnp.arange(deep, dtype=jnp.int32)) % deep
        moved = jnp.take(jnp.stack(moved), order, axis=0, mode="clip")
        moved = moved.transpose(1, 2, 0, 3).reshape(cores, out_rows + 8, width)
        other = shifted(of(moved, 1 - core), "core", cores, 1)
        mine = of(moved, core)
        first = jnp.where(core == 0, mine, other)
        second = jnp.where(core == 0, other, mine)
        moved = jnp.stack([first, second])
        local = moved[:, out_rows]
        total = local
        for shift in range(1, rows):
            total = total + shifted(local, "row", rows, shift)
        return -moved[:, :out_rows], total

    col = ("z", "core")
    in_specs = (P(None, "row", col), P(None, col, None), P(None, "row", None), P())
    out_specs = (P(None, ("row", "z", "core"), None), P())
    return jax.shard_map(
        per_device, mesh=fine, in_specs=in_specs, out_specs=out_specs, check_vma=False
    )
```

```python
import jax
import jax.numpy as jnp
from jax import lax
from jax.sharding import Mesh, PartitionSpec as P

B = 256


def solution(mesh):
    rows, cols = mesh.shape["row"], mesh.shape["col"]
    cores, deep = 2, cols // 2
    fine = Mesh(mesh.devices.reshape(rows, deep, cores), ("row", "z", "core"))
    highest = lax.Precision.HIGHEST

    def shifted(array, axis, size, shift):
        return lax.ppermute(array, axis, [(i, (i + shift) % size) for i in range(size)])

    def gathered(array, axis, size):
        return [array] + [shifted(array, axis, size, d) for d in range(1, size)]

    def per_device(ancestor, panel, factor_inv, pattern):
        row = lax.axis_index("row")
        z = lax.axis_index("z")
        core = lax.axis_index("core")
        _, chunk, width = panel.shape
        depth = factor_inv.shape[1]
        part = width // deep
        piece = chunk // rows
        quarter = cores * piece
        out_rows = ancestor.shape[1] // cols

        def of(array, s):
            return lax.dynamic_index_in_dim(array, s, 0, keepdims=False)

        def swapped(array):
            other = shifted(of(array, 1 - core), "core", cores, 1)
            mine = of(array, core)
            return jnp.stack([jnp.where(core == 0, mine, other), jnp.where(core == 0, other, mine)])

        early = [d for d in range(1, deep) if deep < 4 * d < 3 * deep]
        late = [d for d in range(1, deep) if d not in early]
        far = {d: shifted(ancestor, "z", deep, d) for d in early}

        mine = lax.dynamic_slice_in_dim(panel, row * depth, depth, axis=2)
        partial = jnp.einsum("srw,swv->srv", mine, factor_inv, precision=highest)

        def rows_of(r):
            return lax.dynamic_slice_in_dim(partial, r * piece, piece, axis=1)

        scaled = rows_of(row)
        for shift in range(1, rows):
            scaled = scaled + shifted(rows_of((row + shift) % rows), "row", rows, shift)
        scaled, far = lax.optimization_barrier((swapped(scaled), far))

        def columns_of(array, c):
            return lax.dynamic_slice_in_dim(array, c * part, part, axis=1)

        scaled = scaled.reshape(quarter, width)
        slots = [columns_of(scaled, z)]
        for shift in range(1, deep):
            slots.append(shifted(columns_of(scaled, (z + shift) % deep), "z", deep, shift))
        slots, held_back = lax.optimization_barrier((jnp.stack(slots), ancestor))
        far |= {d: shifted(held_back, "z", deep, d) for d in late}
        slots = jnp.stack(gathered(slots, "row", rows))
        slots = slots.reshape(rows, deep, cores, piece, part)

        place = of(pattern, core)
        stored = jnp.arange(deep, dtype=jnp.int32)
        stored = jnp.sum(jnp.where(place[:, None] == stored[None, :], stored[:, None], 0), axis=0)
        tiles = (z - jnp.arange(deep, dtype=jnp.int32)) % deep
        quarters = (row - jnp.arange(rows, dtype=jnp.int32)) % rows
        from_z = (z - jnp.take(stored, tiles, mode="clip")) % deep
        spread = slots[quarters[None, :], from_z[:, None]]
        spread = spread.transpose(0, 2, 1, 3, 4).reshape(deep, cores, chunk, part)
        wide = jnp.stack([swapped(a) for a in [held_back] + [far[d] for d in range(1, deep)]])
        product = jnp.einsum("tcij,tcjk->ik", wide, spread, precision=highest)
        spread = spread.reshape(deep, B, part)

        held = product.shape[0] // B
        own = jnp.concatenate([of(spread, (z - (row * held + t)) % deep) for t in range(held)])
        term = jnp.sum(own * product, axis=0) + jnp.sum(columns_of(of(factor_inv, core), z) ** 2, axis=0)

        tail = jnp.broadcast_to(term, (cores, 8, part))

        def rows_for(c):
            block = lax.dynamic_slice_in_dim(product, c * cores * out_rows, cores * out_rows)
            block = block.reshape(cores, out_rows, part)
            return jnp.concatenate([block, tail], axis=1)

        moved = [rows_for(z)]
        for shift in range(1, deep):
            moved.append(shifted(rows_for((z + shift) % deep), "z", deep, shift))
        order = (z - jnp.arange(deep, dtype=jnp.int32)) % deep
        moved = jnp.take(jnp.stack(moved), order, axis=0, mode="clip")
        moved = moved.transpose(1, 2, 0, 3).reshape(cores, out_rows + 8, width)
        other = shifted(of(moved, 1 - core), "core", cores, 1)
        mine = of(moved, core)
        first = jnp.where(core == 0, mine, other)
        second = jnp.where(core == 0, other, mine)
        moved = jnp.stack([first, second])
        local = moved[:, out_rows]
        total = local
        for shift in range(1, rows):
            total = total + shifted(local, "row", rows, shift)
        return -moved[:, :out_rows], total

    col = ("z", "core")
    in_specs = (P(None, "row", col), P(None, col, None), P(None, "row", None), P())
    out_specs = (P(None, ("row", "z", "core"), None), P())
    return jax.shard_map(
        per_device, mesh=fine, in_specs=in_specs, out_specs=out_specs, check_vma=False
    )
```

```python
import jax
import jax.numpy as jnp
from jax import lax
from jax.sharding import Mesh, PartitionSpec as P

B = 256


def solution(mesh):
    rows, cols = mesh.shape["row"], mesh.shape["col"]
    cores, deep = 2, cols // 2
    fine = Mesh(mesh.devices.reshape(rows, deep, cores), ("row", "z", "core"))
    highest = lax.Precision.HIGHEST

    def shifted(array, axis, size, shift):
        return lax.ppermute(array, axis, [(i, (i + shift) % size) for i in range(size)])

    def gathered(array, axis, size):
        return [array] + [shifted(array, axis, size, d) for d in range(1, size)]

    def per_device(ancestor, panel, factor_inv, pattern):
        row = lax.axis_index("row")
        z = lax.axis_index("z")
        core = lax.axis_index("core")
        groups, chunk, width = panel.shape
        depth = factor_inv.shape[1]
        part = width // deep
        piece = chunk // rows
        out_rows = ancestor.shape[1] // cols
        tiles = ancestor.shape[1] // B

        def picked(slots, place, at):
            value = slots[0]
            for d in range(1, len(slots)):
                value = jnp.where((place - at) % len(slots) == d, slots[d], value)
            return value

        early = [d for d in range(1, deep) if deep < 4 * d < 3 * deep]
        late = [d for d in range(1, deep) if d not in early]
        far = {d: shifted(ancestor, "z", deep, d) for d in early}

        mine = lax.dynamic_slice_in_dim(panel, row * depth, depth, axis=2)
        partial = jnp.einsum("srw,swv->srv", mine, factor_inv, precision=highest)

        def rows_of(r):
            return lax.dynamic_slice_in_dim(partial, r * piece, piece, axis=1)

        scaled = rows_of(row)
        for shift in range(1, rows):
            scaled = scaled + shifted(rows_of((row + shift) % rows), "row", rows, shift)
        scaled, far = lax.optimization_barrier((scaled, far))

        def columns_of(array, c):
            return lax.dynamic_slice_in_dim(array, c * part, part, axis=2)

        slots = [columns_of(scaled, z)]
        for shift in range(1, deep):
            slots.append(shifted(columns_of(scaled, (z + shift) % deep), "z", deep, shift))
        if deep > 1:
            slots[1], held_back = lax.optimization_barrier((slots[1], ancestor))
            far |= {d: shifted(held_back, "z", deep, d) for d in late}
            slots, far[1] = lax.optimization_barrier((slots, far[1]))
        scaled = jnp.stack(gathered(jnp.stack(slots), "row", rows))

        count = jnp.arange(deep, dtype=jnp.int32)
        stored = jnp.sum(
            jnp.where(pattern[:, :, None] == count, count[:, None], 0), axis=1, dtype=jnp.int32
        )
        from_z = (z - jnp.take(stored, (z - count) % deep, axis=1, mode="clip")) % deep
        from_row = (row - jnp.arange(rows, dtype=jnp.int32)) % rows
        group = jnp.arange(groups, dtype=jnp.int32)
        spread = scaled[from_row, from_z[:, :, None], group[:, None, None]]
        spread = spread.reshape(groups, deep, chunk, part)
        wide = jnp.stack([ancestor] + [far[d] for d in range(1, deep)])
        product = jnp.einsum("dsij,sdjk->sik", wide, spread, precision=highest)
        product = product + shifted(product, "core", cores, 1)

        own = [
            lax.dynamic_index_in_dim(spread, (z - (row * tiles + t)) % deep, 1, keepdims=False)
            for t in range(tiles)
        ]
        own = jnp.stack(own, axis=1)
        other = shifted(own, "core", cores, 1)
        halves = [jnp.where(core == 0, own, other), jnp.where(core == 0, other, own)]
        own = jnp.stack(halves, axis=2).reshape(groups, -1, part)
        squares = jnp.sum(columns_of(factor_inv, z) ** 2, axis=1)
        term = jnp.sum(own * product, axis=1) + squares
        tail = jnp.broadcast_to(term[:, None], (groups, 8, part))

        def rows_for(c):
            block = lax.dynamic_slice_in_dim(product, (c * cores + core) * out_rows, out_rows, axis=1)
            return jnp.concatenate([block, tail], axis=1)

        moved = [rows_for(z)]
        for shift in range(1, deep):
            moved.append(shifted(rows_for((z + shift) % deep), "z", deep, shift))
        moved = jnp.concatenate([picked(moved, z, c) for c in range(deep)], axis=2)
        local = moved[:, out_rows]
        total = local
        for shift in range(1, rows):
            total = total + shifted(local, "row", rows, shift)
        return -moved[:, :out_rows], total

    col = ("z", "core")
    in_specs = (P(None, "row", col), P(None, col, None), P(None, "row", None), P())
    out_specs = (P(None, ("row", "z", "core"), None), P())
    return jax.shard_map(
        per_device, mesh=fine, in_specs=in_specs, out_specs=out_specs, check_vma=False
    )
```

```python
import jax
import jax.numpy as jnp
from jax import lax
from jax.sharding import Mesh, PartitionSpec as P

B = 256


def solution(mesh):
    rows, cols = mesh.shape["row"], mesh.shape["col"]
    cores, deep = 2, cols // 2
    fine = Mesh(mesh.devices.reshape(rows, deep, cores), ("row", "z", "core"))
    highest = lax.Precision.HIGHEST

    def shifted(array, axis, size, shift):
        return lax.ppermute(array, axis, [(i, (i + shift) % size) for i in range(size)])

    def gathered(array, axis, size):
        return [array] + [shifted(array, axis, size, d) for d in range(1, size)]

    def per_device(ancestor, panel, factor_inv, pattern):
        row = lax.axis_index("row")
        z = lax.axis_index("z")
        core = lax.axis_index("core")
        groups, chunk, width = panel.shape
        depth = factor_inv.shape[1]
        part = width // deep
        piece = chunk // rows
        out_rows = ancestor.shape[1] // cols
        tiles = ancestor.shape[1] // B

        def picked(slots, place, at):
            value = slots[0]
            for d in range(1, len(slots)):
                value = jnp.where((place - at) % len(slots) == d, slots[d], value)
            return value

        def passed(piece, step):
            pairs = [(i, i + step) for i in range(deep) if 0 <= i + step < deep]
            return lax.ppermute(piece, "z", pairs)

        before, after = [ancestor], [ancestor]

        def pass_on():
            if len(before) < deep:
                before.append(passed(before[-1], 1))
                after.append(passed(after[-1], -1))

        pass_on()

        mine = lax.dynamic_slice_in_dim(panel, row * depth, depth, axis=2)
        partial = jnp.einsum("srw,swv->srv", mine, factor_inv, precision=highest)

        def rows_of(r):
            return lax.dynamic_slice_in_dim(partial, r * piece, piece, axis=1)

        scaled = rows_of(row)
        for shift in range(1, rows):
            scaled = scaled + shifted(rows_of((row + shift) % rows), "row", rows, shift)
        scaled, before[-1], after[-1] = lax.optimization_barrier((scaled, before[-1], after[-1]))
        pass_on()

        def columns_of(array, c):
            return lax.dynamic_slice_in_dim(array, c * part, part, axis=2)

        slots = [columns_of(scaled, z)]
        for shift in range(1, deep):
            slots.append(shifted(columns_of(scaled, (z + shift) % deep), "z", deep, shift))
        slots, before[-1], after[-1] = lax.optimization_barrier((slots, before[-1], after[-1]))
        while len(before) < deep:
            pass_on()
        scaled = jnp.stack(gathered(jnp.stack(slots), "row", rows))

        count = jnp.arange(deep, dtype=jnp.int32)
        stored = jnp.sum(
            jnp.where(pattern[:, :, None] == count, count[:, None], 0), axis=1, dtype=jnp.int32
        )
        from_z = (z - jnp.take(stored, (z - count) % deep, axis=1, mode="clip")) % deep
        from_row = (row - jnp.arange(rows, dtype=jnp.int32)) % rows
        group = jnp.arange(groups, dtype=jnp.int32)
        spread = scaled[from_row, from_z[:, :, None], group[:, None, None]]
        spread = spread.reshape(groups, deep, chunk, part)
        far = [jnp.where(z >= d, before[d], after[deep - d]) for d in range(1, deep)]
        wide = jnp.stack([ancestor] + far)
        product = jnp.einsum("dsij,sdjk->sik", wide, spread, precision=highest)
        product = product + shifted(product, "core", cores, 1)

        own = [
            lax.dynamic_index_in_dim(spread, (z - (row * tiles + t)) % deep, 1, keepdims=False)
            for t in range(tiles)
        ]
        own = jnp.stack(own, axis=1)
        other = shifted(own, "core", cores, 1)
        halves = [jnp.where(core == 0, own, other), jnp.where(core == 0, other, own)]
        own = jnp.stack(halves, axis=2).reshape(groups, -1, part)
        squares = jnp.sum(columns_of(factor_inv, z) ** 2, axis=1)
        term = jnp.sum(own * product, axis=1) + squares
        tail = jnp.broadcast_to(term[:, None], (groups, 8, part))

        def rows_for(c):
            block = lax.dynamic_slice_in_dim(product, (c * cores + core) * out_rows, out_rows, axis=1)
            return jnp.concatenate([block, tail], axis=1)

        moved = [rows_for(z)]
        for shift in range(1, deep):
            moved.append(shifted(rows_for((z + shift) % deep), "z", deep, shift))
        moved = jnp.concatenate([picked(moved, z, c) for c in range(deep)], axis=2)
        local = moved[:, out_rows]
        total = local
        for shift in range(1, rows):
            total = total + shifted(local, "row", rows, shift)
        return -moved[:, :out_rows], total

    col = ("z", "core")
    in_specs = (P(None, "row", col), P(None, col, None), P(None, "row", None), P())
    out_specs = (P(None, ("row", "z", "core"), None), P())
    return jax.shard_map(
        per_device, mesh=fine, in_specs=in_specs, out_specs=out_specs, check_vma=False
    )
```

```python
import functools

import jax
import jax.numpy as jnp
from jax import lax
from jax.experimental import pallas as pl
from jax.experimental.pallas import tpu as pltpu
from jax.sharding import Mesh, PartitionSpec as P

B = 256


def multiply_tiles(deep, rows, place, *refs):
    far, slots, (out_ref, spread) = refs[:deep], refs[deep : deep + rows], refs[deep + rows :]
    groups, height, chunk = far[0].shape
    piece = slots[0].shape[2]
    for s in range(groups):
        for d in range(deep):
            slot = place[s * deep + d]
            for e in range(rows):
                first = pl.multiple_of(place[groups * deep + e] * piece, piece)
                spread[s, d, pl.ds(first, piece)] = slots[e][slot, s]
    tiles = (out_ref.shape[1] - height) // chunk
    for s in range(groups):
        wide = jnp.concatenate([piece_ref[s] for piece_ref in far], axis=1)
        tall = spread[s].reshape(deep * chunk, spread.shape[3])
        out_ref[s, :height] = jnp.dot(
            wide, tall, precision=lax.Precision.HIGHEST, preferred_element_type=jnp.float32
        )
        for t in range(tiles):
            own = spread[s, place[groups * deep + rows + t]]
            out_ref[s, height + t * chunk : height + (t + 1) * chunk] = own


def solution(mesh):
    rows, cols = mesh.shape["row"], mesh.shape["col"]
    cores, deep = 2, cols // 2
    fine = Mesh(mesh.devices.reshape(rows, deep, cores), ("row", "z", "core"))
    highest = lax.Precision.HIGHEST

    def shifted(array, axis, size, shift):
        return lax.ppermute(array, axis, [(i, (i + shift) % size) for i in range(size)])

    def gathered(array, axis, size):
        return [array] + [shifted(array, axis, size, d) for d in range(1, size)]

    def per_device(ancestor, panel, factor_inv, pattern):
        row = lax.axis_index("row")
        z = lax.axis_index("z")
        core = lax.axis_index("core")
        groups, chunk, width = panel.shape
        depth = factor_inv.shape[1]
        part = width // deep
        piece = chunk // rows
        out_rows = ancestor.shape[1] // cols
        tiles = ancestor.shape[1] // B

        def picked(slots, place, at):
            value = slots[0]
            for d in range(1, len(slots)):
                value = jnp.where((place - at) % len(slots) == d, slots[d], value)
            return value

        early = [d for d in range(1, deep) if deep < 4 * d < 3 * deep]
        late = [d for d in range(1, deep) if d not in early]
        far = {d: shifted(ancestor, "z", deep, d) for d in early}

        mine = lax.dynamic_slice_in_dim(panel, row * depth, depth, axis=2)
        partial = jnp.einsum("srw,swv->srv", mine, factor_inv, precision=highest)

        def rows_of(r):
            return lax.dynamic_slice_in_dim(partial, r * piece, piece, axis=1)

        sums = [shifted(rows_of((row + d) % rows), "row", rows, d) for d in range(1, rows)]
        sums[0], far = lax.optimization_barrier((sums[0], far))
        scaled = sum(sums, rows_of(row))

        def columns_of(array, c):
            return lax.dynamic_slice_in_dim(array, c * part, part, axis=2)

        slots = [columns_of(scaled, z)]
        for shift in range(1, deep):
            slots.append(shifted(columns_of(scaled, (z + shift) % deep), "z", deep, shift))
        if deep > 1:
            slots[1], held_back = lax.optimization_barrier((slots[1], ancestor))
            far |= {d: shifted(held_back, "z", deep, d) for d in late}
        slots = gathered(jnp.stack(slots), "row", rows)

        count = jnp.arange(deep, dtype=jnp.int32)
        at = (z - count) % deep
        stored = jnp.sum(
            jnp.where(pattern[:, :, None] == at, count[:, None], 0), axis=1, dtype=jnp.int32
        )
        from_z = ((z - stored) % deep).reshape(-1)
        quarter = (row - jnp.arange(rows, dtype=jnp.int32)) % rows
        own_tile = (z - row * tiles - jnp.arange(tiles, dtype=jnp.int32)) % deep
        place = jnp.concatenate([from_z, quarter, own_tile])
        height = ancestor.shape[1]
        whole = pl.BlockSpec(memory_space=pltpu.VMEM)
        product = pl.pallas_call(
            functools.partial(multiply_tiles, deep, rows),
            out_shape=jax.ShapeDtypeStruct((groups, height + tiles * chunk, part), jnp.float32),
            in_specs=[pl.BlockSpec(memory_space=pltpu.SMEM)] + [whole] * (deep + rows),
            out_specs=whole,
            scratch_shapes=[pltpu.VMEM((groups, deep, chunk, part), jnp.float32)],
            compiler_params=pltpu.CompilerParams(vmem_limit_bytes=32 * 1024 * 1024),
        )(place, ancestor, *[far[d] for d in range(1, deep)], *slots)
        other = shifted(product, "core", cores, 1)

        own, own_other = [
            array[:, height:].reshape(groups, tiles, chunk, part) for array in (product, other)
        ]
        product = product[:, :height] + other[:, :height]
        halves = [jnp.where(core == 0, own, own_other), jnp.where(core == 0, own_other, own)]
        own = jnp.stack(halves, axis=2).reshape(groups, height, part)
        squares = jnp.sum(columns_of(factor_inv, z) ** 2, axis=1)
        term = jnp.sum(own * product, axis=1) + squares
        tail = jnp.broadcast_to(term[:, None], (groups, 8, part))

        def rows_for(c):
            block = lax.dynamic_slice_in_dim(product, (c * cores + core) * out_rows, out_rows, axis=1)
            return jnp.concatenate([block, tail], axis=1)

        moved = [rows_for(z)]
        for shift in range(1, deep):
            moved.append(shifted(rows_for((z + shift) % deep), "z", deep, shift))
        moved = jnp.concatenate([picked(moved, z, c) for c in range(deep)], axis=2)
        local = moved[:, out_rows]
        total = local
        for shift in range(1, rows):
            total = total + shifted(local, "row", rows, shift)
        return -moved[:, :out_rows], total

    col = ("z", "core")
    in_specs = (P(None, "row", col), P(None, col, None), P(None, "row", None), P())
    out_specs = (P(None, ("row", "z", "core"), None), P())
    return jax.shard_map(
        per_device, mesh=fine, in_specs=in_specs, out_specs=out_specs, check_vma=False
    )
```

```python
import functools

import jax
import jax.numpy as jnp
from jax import lax
from jax.experimental import pallas as pl
from jax.experimental.pallas import tpu as pltpu
from jax.sharding import Mesh, PartitionSpec as P

B = 256


def multiply_tiles(deep, rows, place, *refs):
    far, slots, (out_ref, spread) = refs[:deep], refs[deep : deep + rows], refs[deep + rows :]
    groups, height, chunk = far[0].shape
    piece = slots[0].shape[2]
    for s in range(groups):
        for d in range(deep):
            slot = place[s * deep + d]
            for e in range(rows):
                first = pl.multiple_of(place[groups * deep + e] * piece, piece)
                spread[s, d, pl.ds(first, piece)] = slots[e][slot, s]
    tiles = (out_ref.shape[1] - height) // chunk
    for s in range(groups):
        wide = jnp.concatenate([piece_ref[s] for piece_ref in far], axis=1)
        tall = spread[s].reshape(deep * chunk, spread.shape[3])
        out_ref[s, :height] = jnp.dot(
            wide, tall, precision=lax.Precision.HIGHEST, preferred_element_type=jnp.float32
        )
        for t in range(tiles):
            own = spread[s, place[groups * deep + rows + t]]
            out_ref[s, height + t * chunk : height + (t + 1) * chunk] = own


def solution(mesh):
    rows, cols = mesh.shape["row"], mesh.shape["col"]
    cores, deep = 2, cols // 2
    fine = Mesh(mesh.devices.reshape(rows, deep, cores), ("row", "z", "core"))
    highest = lax.Precision.HIGHEST

    def shifted(array, axis, size, shift):
        return lax.ppermute(array, axis, [(i, (i + shift) % size) for i in range(size)])

    def gathered(array, axis, size):
        return [array] + [shifted(array, axis, size, d) for d in range(1, size)]

    def per_device(ancestor, panel, factor_inv, pattern):
        row = lax.axis_index("row")
        z = lax.axis_index("z")
        core = lax.axis_index("core")
        groups, chunk, width = panel.shape
        depth = factor_inv.shape[1]
        part = width // deep
        piece = chunk // rows
        out_rows = ancestor.shape[1] // cols
        tiles = ancestor.shape[1] // B

        def picked(slots, place, at):
            value = slots[0]
            for d in range(1, len(slots)):
                value = jnp.where((place - at) % len(slots) == d, slots[d], value)
            return value

        early = [d for d in range(1, deep) if deep < 4 * d < 3 * deep]
        late = [d for d in range(1, deep) if d not in early]
        far = {d: shifted(ancestor, "z", deep, d) for d in early}

        mine = lax.dynamic_slice_in_dim(panel, row * depth, depth, axis=2)
        partial = jnp.einsum("srw,swv->srv", mine, factor_inv, precision=highest)

        def rows_of(r):
            return lax.dynamic_slice_in_dim(partial, r * piece, piece, axis=1)

        sums = [shifted(rows_of((row + d) % rows), "row", rows, d) for d in range(1, rows)]
        scaled = sum(sums, rows_of(row))

        def columns_of(array, c):
            return lax.dynamic_slice_in_dim(array, c * part, part, axis=2)

        slots = [columns_of(scaled, z)]
        for shift in range(1, deep):
            slots.append(shifted(columns_of(scaled, (z + shift) % deep), "z", deep, shift))
        if deep > 1:
            slots[1], held_back = lax.optimization_barrier((slots[1], ancestor))
            far |= {d: shifted(held_back, "z", deep, d) for d in late}
        slots = gathered(jnp.stack(slots), "row", rows)

        count = jnp.arange(deep, dtype=jnp.int32)
        at = (z - count) % deep
        stored = jnp.sum(
            jnp.where(pattern[:, :, None] == at, count[:, None], 0), axis=1, dtype=jnp.int32
        )
        from_z = ((z - stored) % deep).reshape(-1)
        quarter = (row - jnp.arange(rows, dtype=jnp.int32)) % rows
        own_tile = (z - row * tiles - jnp.arange(tiles, dtype=jnp.int32)) % deep
        place = jnp.concatenate([from_z, quarter, own_tile])
        height = ancestor.shape[1]
        whole = pl.BlockSpec(memory_space=pltpu.VMEM)
        product = pl.pallas_call(
            functools.partial(multiply_tiles, deep, rows),
            out_shape=jax.ShapeDtypeStruct((groups, height + tiles * chunk, part), jnp.float32),
            in_specs=[pl.BlockSpec(memory_space=pltpu.SMEM)] + [whole] * (deep + rows),
            out_specs=whole,
            scratch_shapes=[pltpu.VMEM((groups, deep, chunk, part), jnp.float32)],
            compiler_params=pltpu.CompilerParams(vmem_limit_bytes=32 * 1024 * 1024),
        )(place, ancestor, *[far[d] for d in range(1, deep)], *slots)
        other = shifted(product, "core", cores, 1)

        own, own_other = [
            array[:, height:].reshape(groups, tiles, chunk, part) for array in (product, other)
        ]
        product = product[:, :height] + other[:, :height]
        halves = [jnp.where(core == 0, own, own_other), jnp.where(core == 0, own_other, own)]
        own = jnp.stack(halves, axis=2).reshape(groups, height, part)
        squares = jnp.sum(columns_of(factor_inv, z) ** 2, axis=1)
        term = jnp.sum(own * product, axis=1) + squares
        tail = jnp.broadcast_to(term[:, None], (groups, 8, part))

        def rows_for(c):
            block = lax.dynamic_slice_in_dim(product, (c * cores + core) * out_rows, out_rows, axis=1)
            return jnp.concatenate([block, tail], axis=1)

        moved = [rows_for(z)]
        for shift in range(1, deep):
            moved.append(shifted(rows_for((z + shift) % deep), "z", deep, shift))
        moved = jnp.concatenate([picked(moved, z, c) for c in range(deep)], axis=2)
        local = moved[:, out_rows]
        total = local
        for shift in range(1, rows):
            total = total + shifted(local, "row", rows, shift)
        return -moved[:, :out_rows], total

    col = ("z", "core")
    in_specs = (P(None, "row", col), P(None, col, None), P(None, "row", None), P())
    out_specs = (P(None, ("row", "z", "core"), None), P())
    return jax.shard_map(
        per_device, mesh=fine, in_specs=in_specs, out_specs=out_specs, check_vma=False
    )
```

```python
import functools

import jax
import jax.numpy as jnp
from jax import lax
from jax.experimental import pallas as pl
from jax.experimental.pallas import tpu as pltpu
from jax.sharding import Mesh, PartitionSpec as P

B = 256


def multiply_tiles(deep, rows, place, *refs):
    far, slots, (out_ref, spread) = refs[:deep], refs[deep : deep + rows], refs[deep + rows :]
    groups, height, chunk = far[0].shape
    piece = slots[0].shape[2]
    for s in range(groups):
        for d in range(deep):
            slot = place[s * deep + d]
            for e in range(rows):
                first = pl.multiple_of(place[groups * deep + e] * piece, piece)
                spread[s, d, pl.ds(first, piece)] = slots[e][slot, s]
    tiles = (out_ref.shape[1] - height) // chunk
    for s in range(groups):
        wide = jnp.concatenate([piece_ref[s] for piece_ref in far], axis=1)
        tall = spread[s].reshape(deep * chunk, spread.shape[3])
        out_ref[s, :height] = jnp.dot(
            wide, tall, precision=lax.Precision.HIGHEST, preferred_element_type=jnp.float32
        )
        for t in range(tiles):
            own = spread[s, place[groups * deep + rows + t]]
            out_ref[s, height + t * chunk : height + (t + 1) * chunk] = own


def solution(mesh):
    rows, cols = mesh.shape["row"], mesh.shape["col"]
    cores, deep = 2, cols // 2
    fine = Mesh(mesh.devices.reshape(rows, deep, cores), ("row", "z", "core"))
    highest = lax.Precision.HIGHEST

    def shifted(array, axis, size, shift):
        return lax.ppermute(array, axis, [(i, (i + shift) % size) for i in range(size)])

    def gathered(array, axis, size):
        return [array] + [shifted(array, axis, size, d) for d in range(1, size)]

    def per_device(ancestor, panel, factor_inv, pattern):
        row = lax.axis_index("row")
        z = lax.axis_index("z")
        core = lax.axis_index("core")
        groups, chunk, width = panel.shape
        depth = factor_inv.shape[1]
        part = width // deep
        piece = chunk // rows
        out_rows = ancestor.shape[1] // cols
        tiles = ancestor.shape[1] // B

        def picked(slots, place, at):
            value = slots[0]
            for d in range(1, len(slots)):
                value = jnp.where((place - at) % len(slots) == d, slots[d], value)
            return value

        early = [d for d in range(1, deep) if not deep < 4 * d < 3 * deep]
        late = [d for d in range(1, deep) if d not in early]
        far = {d: shifted(ancestor, "z", deep, d) for d in early}

        mine = lax.dynamic_slice_in_dim(panel, row * depth, depth, axis=2)
        partial = jnp.einsum("srw,swv->srv", mine, factor_inv, precision=highest)

        def rows_of(r):
            return lax.dynamic_slice_in_dim(partial, r * piece, piece, axis=1)

        sums = [shifted(rows_of((row + d) % rows), "row", rows, d) for d in range(1, rows)]
        sums, far = lax.optimization_barrier((sums, far))
        scaled = sum(sums, rows_of(row))

        def columns_of(array, c):
            return lax.dynamic_slice_in_dim(array, c * part, part, axis=2)

        slots = [columns_of(scaled, z)]
        for shift in range(1, deep):
            slots.append(shifted(columns_of(scaled, (z + shift) % deep), "z", deep, shift))
        if deep > 1:
            slots[1], held_back = lax.optimization_barrier((slots[1], ancestor))
            far |= {d: shifted(held_back, "z", deep, d) for d in late}
        slots = gathered(jnp.stack(slots), "row", rows)

        count = jnp.arange(deep, dtype=jnp.int32)
        at = (z - count) % deep
        stored = jnp.sum(
            jnp.where(pattern[:, :, None] == at, count[:, None], 0), axis=1, dtype=jnp.int32
        )
        from_z = ((z - stored) % deep).reshape(-1)
        quarter = (row - jnp.arange(rows, dtype=jnp.int32)) % rows
        own_tile = (z - row * tiles - jnp.arange(tiles, dtype=jnp.int32)) % deep
        place = jnp.concatenate([from_z, quarter, own_tile])
        height = ancestor.shape[1]
        whole = pl.BlockSpec(memory_space=pltpu.VMEM)
        product = pl.pallas_call(
            functools.partial(multiply_tiles, deep, rows),
            out_shape=jax.ShapeDtypeStruct((groups, height + tiles * chunk, part), jnp.float32),
            in_specs=[pl.BlockSpec(memory_space=pltpu.SMEM)] + [whole] * (deep + rows),
            out_specs=whole,
            scratch_shapes=[pltpu.VMEM((groups, deep, chunk, part), jnp.float32)],
            compiler_params=pltpu.CompilerParams(vmem_limit_bytes=32 * 1024 * 1024),
        )(place, ancestor, *[far[d] for d in range(1, deep)], *slots)
        other = shifted(product, "core", cores, 1)

        own, own_other = [
            array[:, height:].reshape(groups, tiles, chunk, part) for array in (product, other)
        ]
        product = product[:, :height] + other[:, :height]
        halves = [jnp.where(core == 0, own, own_other), jnp.where(core == 0, own_other, own)]
        own = jnp.stack(halves, axis=2).reshape(groups, height, part)
        squares = jnp.sum(columns_of(factor_inv, z) ** 2, axis=1)
        term = jnp.sum(own * product, axis=1) + squares
        tail = jnp.broadcast_to(term[:, None], (groups, 8, part))

        def rows_for(c):
            block = lax.dynamic_slice_in_dim(product, (c * cores + core) * out_rows, out_rows, axis=1)
            return jnp.concatenate([block, tail], axis=1)

        moved = [rows_for(z)]
        for shift in range(1, deep):
            moved.append(shifted(rows_for((z + shift) % deep), "z", deep, shift))
        moved = jnp.concatenate([picked(moved, z, c) for c in range(deep)], axis=2)
        local = moved[:, out_rows]
        total = local
        for shift in range(1, rows):
            total = total + shifted(local, "row", rows, shift)
        return -moved[:, :out_rows], total

    col = ("z", "core")
    in_specs = (P(None, "row", col), P(None, col, None), P(None, "row", None), P())
    out_specs = (P(None, ("row", "z", "core"), None), P())
    return jax.shard_map(
        per_device, mesh=fine, in_specs=in_specs, out_specs=out_specs, check_vma=False
    )
```

```python
import functools

import jax
import jax.numpy as jnp
from jax import lax
from jax.experimental import pallas as pl
from jax.experimental.pallas import tpu as pltpu
from jax.sharding import Mesh, PartitionSpec as P

B = 256


def multiply_tiles(deep, rows, place, *refs):
    far, slots, (out_ref, spread) = refs[:deep], refs[deep : deep + rows], refs[deep + rows :]
    groups, height, chunk = far[0].shape
    piece = slots[0].shape[2]
    for s in range(groups):
        for d in range(deep):
            slot = place[s * deep + d]
            for e in range(rows):
                first = pl.multiple_of(place[groups * deep + e] * piece, piece)
                spread[s, d, pl.ds(first, piece)] = slots[e][slot, s]
    tiles = (out_ref.shape[1] - height) // chunk
    for s in range(groups):
        wide = jnp.concatenate([piece_ref[s] for piece_ref in far], axis=1)
        tall = spread[s].reshape(deep * chunk, spread.shape[3])
        out_ref[s, :height] = jnp.dot(
            wide, tall, precision=lax.Precision.HIGHEST, preferred_element_type=jnp.float32
        )
        for t in range(tiles):
            own = spread[s, place[groups * deep + rows + t]]
            out_ref[s, height + t * chunk : height + (t + 1) * chunk] = own


def solution(mesh):
    rows, cols = mesh.shape["row"], mesh.shape["col"]
    cores, deep = 2, cols // 2
    fine = Mesh(mesh.devices.reshape(rows, deep, cores), ("row", "z", "core"))
    highest = lax.Precision.HIGHEST

    def shifted(array, axis, size, shift):
        return lax.ppermute(array, axis, [(i, (i + shift) % size) for i in range(size)])

    def gathered(array, axis, size):
        return [array] + [shifted(array, axis, size, d) for d in range(1, size)]

    def per_device(ancestor, panel, factor_inv, pattern):
        row = lax.axis_index("row")
        z = lax.axis_index("z")
        core = lax.axis_index("core")
        groups, chunk, width = panel.shape
        depth = factor_inv.shape[1]
        part = width // deep
        piece = chunk // rows
        out_rows = ancestor.shape[1] // cols
        tiles = ancestor.shape[1] // B

        def picked(slots, place, at):
            value = slots[0]
            for d in range(1, len(slots)):
                value = jnp.where((place - at) % len(slots) == d, slots[d], value)
            return value

        early = [d for d in range(1, deep) if not deep < 4 * d < 3 * deep]
        late = [d for d in range(1, deep) if d not in early]
        far = {d: shifted(ancestor, "z", deep, d) for d in early}

        mine = lax.dynamic_slice_in_dim(panel, row * depth, depth, axis=2)
        partial = jnp.einsum("srw,swv->srv", mine, factor_inv, precision=highest)

        def rows_of(r):
            return lax.dynamic_slice_in_dim(partial, r * piece, piece, axis=1)

        sums = [shifted(rows_of((row + d) % rows), "row", rows, d) for d in range(1, rows)]
        sums, far = lax.optimization_barrier((sums, far))
        scaled = sum(sums, rows_of(row))

        def columns_of(array, c):
            return lax.dynamic_slice_in_dim(array, c * part, part, axis=2)

        slots = [columns_of(scaled, z)]
        for shift in range(1, deep):
            slots.append(shifted(columns_of(scaled, (z + shift) % deep), "z", deep, shift))
        if deep > 1:
            slots, far[1] = lax.optimization_barrier((slots, far[1]))
            for d in late:
                far[d] = shifted(far[d - 1], "z", deep, 1)
        slots = gathered(jnp.stack(slots), "row", rows)

        count = jnp.arange(deep, dtype=jnp.int32)
        at = (z - count) % deep
        stored = jnp.sum(
            jnp.where(pattern[:, :, None] == at, count[:, None], 0), axis=1, dtype=jnp.int32
        )
        from_z = ((z - stored) % deep).reshape(-1)
        quarter = (row - jnp.arange(rows, dtype=jnp.int32)) % rows
        own_tile = (z - row * tiles - jnp.arange(tiles, dtype=jnp.int32)) % deep
        place = jnp.concatenate([from_z, quarter, own_tile])
        height = ancestor.shape[1]
        whole = pl.BlockSpec(memory_space=pltpu.VMEM)
        product = pl.pallas_call(
            functools.partial(multiply_tiles, deep, rows),
            out_shape=jax.ShapeDtypeStruct((groups, height + tiles * chunk, part), jnp.float32),
            in_specs=[pl.BlockSpec(memory_space=pltpu.SMEM)] + [whole] * (deep + rows),
            out_specs=whole,
            scratch_shapes=[pltpu.VMEM((groups, deep, chunk, part), jnp.float32)],
            compiler_params=pltpu.CompilerParams(vmem_limit_bytes=32 * 1024 * 1024),
        )(place, ancestor, *[far[d] for d in range(1, deep)], *slots)
        other = shifted(product, "core", cores, 1)

        own, own_other = [
            array[:, height:].reshape(groups, tiles, chunk, part) for array in (product, other)
        ]
        product = product[:, :height] + other[:, :height]
        halves = [jnp.where(core == 0, own, own_other), jnp.where(core == 0, own_other, own)]
        own = jnp.stack(halves, axis=2).reshape(groups, height, part)
        squares = jnp.sum(columns_of(factor_inv, z) ** 2, axis=1)
        term = jnp.sum(own * product, axis=1) + squares
        tail = jnp.broadcast_to(term[:, None], (groups, 8, part))

        def rows_for(c):
            block = lax.dynamic_slice_in_dim(product, (c * cores + core) * out_rows, out_rows, axis=1)
            return jnp.concatenate([block, tail], axis=1)

        moved = [rows_for(z)]
        for shift in range(1, deep):
            moved.append(shifted(rows_for((z + shift) % deep), "z", deep, shift))
        moved = jnp.concatenate([picked(moved, z, c) for c in range(deep)], axis=2)
        local = moved[:, out_rows]
        total = local
        for shift in range(1, rows):
            total = total + shifted(local, "row", rows, shift)
        return -moved[:, :out_rows], total

    col = ("z", "core")
    in_specs = (P(None, "row", col), P(None, col, None), P(None, "row", None), P())
    out_specs = (P(None, ("row", "z", "core"), None), P())
    return jax.shard_map(
        per_device, mesh=fine, in_specs=in_specs, out_specs=out_specs, check_vma=False
    )
```

```python
import functools

import jax
import jax.numpy as jnp
from jax import lax
from jax.experimental import pallas as pl
from jax.experimental.pallas import tpu as pltpu
from jax.sharding import Mesh, PartitionSpec as P

B = 256


def scale_pieces(deep, *refs):
    panels, (factor, out_ref) = refs[:deep], refs[deep:]
    groups, piece, _ = panels[0].shape
    for s in range(groups):
        tall = jnp.concatenate([panel[s] for panel in panels], axis=0)
        scaled = jnp.dot(
            tall, factor[s], precision=lax.Precision.HIGHEST, preferred_element_type=jnp.float32
        )
        for d in range(deep):
            out_ref[d, s] = scaled[d * piece : (d + 1) * piece]


def multiply_tiles(deep, rows, place, *refs):
    far, slots, (out_ref, spread) = refs[:deep], refs[deep : deep + rows], refs[deep + rows :]
    groups, height, chunk = far[0].shape
    piece = slots[0].shape[2]
    for s in range(groups):
        for d in range(deep):
            slot = place[s * deep + d]
            for e in range(rows):
                first = pl.multiple_of(place[groups * deep + e] * piece, piece)
                spread[s, d, pl.ds(first, piece)] = slots[e][slot, s]
    tiles = (out_ref.shape[1] - height) // chunk
    for s in range(groups):
        wide = jnp.concatenate([piece_ref[s] for piece_ref in far], axis=1)
        tall = spread[s].reshape(deep * chunk, spread.shape[3])
        out_ref[s, :height] = jnp.dot(
            wide, tall, precision=lax.Precision.HIGHEST, preferred_element_type=jnp.float32
        )
        for t in range(tiles):
            own = spread[s, place[groups * deep + rows + t]]
            out_ref[s, height + t * chunk : height + (t + 1) * chunk] = own


def solution(mesh):
    rows, cols = mesh.shape["row"], mesh.shape["col"]
    cores, deep = 2, cols // 2
    fine = Mesh(mesh.devices.reshape(rows, deep, cores), ("row", "z", "core"))
    highest = lax.Precision.HIGHEST

    def shifted(array, axis, size, shift):
        return lax.ppermute(array, axis, [(i, (i + shift) % size) for i in range(size)])

    def gathered(array, axis, size):
        return [array] + [shifted(array, axis, size, d) for d in range(1, size)]

    def per_device(ancestor, panel, factor_inv, pattern):
        row = lax.axis_index("row")
        z = lax.axis_index("z")
        core = lax.axis_index("core")
        groups, chunk, width = panel.shape
        part = width // deep
        piece = chunk // rows
        out_rows = ancestor.shape[1] // cols
        tiles = ancestor.shape[1] // B

        def picked(slots, place, at):
            value = slots[0]
            for d in range(1, len(slots)):
                value = jnp.where((place - at) % len(slots) == d, slots[d], value)
            return value

        early = [d for d in range(1, deep) if not deep < 4 * d < 3 * deep]
        late = [d for d in range(1, deep) if d not in early]
        far = {d: shifted(ancestor, "z", deep, d) for d in early}

        whole = pl.BlockSpec(memory_space=pltpu.VMEM)
        scalars = pl.BlockSpec(memory_space=pltpu.SMEM)
        params = pltpu.CompilerParams(vmem_limit_bytes=32 * 1024 * 1024)
        quarter = (row - jnp.arange(rows, dtype=jnp.int32)) % rows

        mine = lax.dynamic_slice_in_dim(panel, row * piece, piece, axis=1)
        block = lax.dynamic_slice_in_dim(factor_inv, z * part, part, axis=2)
        panels = gathered(mine, "z", deep)
        blocks = lax.all_gather(block, "row", axis=1, tiled=True)
        scaled = pl.pallas_call(
            functools.partial(scale_pieces, deep),
            out_shape=jax.ShapeDtypeStruct((deep, groups, piece, part), jnp.float32),
            in_specs=[whole] * (deep + 1),
            out_specs=whole,
            compiler_params=params,
        )(*panels, blocks)
        for d in late:
            far[d] = shifted(far[d - 1], "z", deep, 1)
        slots = gathered(scaled, "row", rows)

        count = jnp.arange(deep, dtype=jnp.int32)
        at = (z - count) % deep
        stored = jnp.sum(
            jnp.where(pattern[:, :, None] == at, count[:, None], 0), axis=1, dtype=jnp.int32
        )
        from_z = ((z - stored) % deep).reshape(-1)
        own_tile = (z - row * tiles - jnp.arange(tiles, dtype=jnp.int32)) % deep
        place = jnp.concatenate([from_z, quarter, own_tile])
        height = ancestor.shape[1]
        product = pl.pallas_call(
            functools.partial(multiply_tiles, deep, rows),
            out_shape=jax.ShapeDtypeStruct((groups, height + tiles * chunk, part), jnp.float32),
            in_specs=[scalars] + [whole] * (deep + rows),
            out_specs=whole,
            scratch_shapes=[pltpu.VMEM((groups, deep, chunk, part), jnp.float32)],
            compiler_params=params,
        )(place, ancestor, *[far[d] for d in range(1, deep)], *slots)
        other = shifted(product, "core", cores, 1)

        own, own_other = [
            array[:, height:].reshape(groups, tiles, chunk, part) for array in (product, other)
        ]
        product = product[:, :height] + other[:, :height]
        halves = [jnp.where(core == 0, own, own_other), jnp.where(core == 0, own_other, own)]
        own = jnp.stack(halves, axis=2).reshape(groups, height, part)
        squares = jnp.sum(block * block, axis=1)
        term = jnp.sum(own * product, axis=1) + squares
        tail = jnp.broadcast_to(term[:, None], (groups, 8, part))

        def rows_for(c):
            block = lax.dynamic_slice_in_dim(product, (c * cores + core) * out_rows, out_rows, axis=1)
            return jnp.concatenate([block, tail], axis=1)

        moved = [rows_for(z)]
        for shift in range(1, deep):
            moved.append(shifted(rows_for((z + shift) % deep), "z", deep, shift))
        moved = jnp.concatenate([picked(moved, z, c) for c in range(deep)], axis=2)
        local = moved[:, out_rows]
        total = local
        for shift in range(1, rows):
            total = total + shifted(local, "row", rows, shift)
        return -moved[:, :out_rows], total

    col = ("z", "core")
    in_specs = (P(None, "row", col), P(None, col, None), P(None, "row", None), P())
    out_specs = (P(None, ("row", "z", "core"), None), P())
    return jax.shard_map(
        per_device, mesh=fine, in_specs=in_specs, out_specs=out_specs, check_vma=False
    )
```

```python
import functools

import jax
import jax.numpy as jnp
from jax import lax
from jax.experimental import pallas as pl
from jax.experimental.pallas import tpu as pltpu
from jax.sharding import Mesh, PartitionSpec as P

B = 256


def scale_pieces(deep, rows, place, *refs):
    panels, blocks, (out_ref, factor) = refs[:deep], refs[deep : deep + rows], refs[deep + rows :]
    groups, piece, _ = panels[0].shape
    depth = blocks[0].shape[1]
    for e in range(rows):
        first = pl.multiple_of(place[e] * depth, depth)
        factor[:, pl.ds(first, depth)] = blocks[e][...]
    for s in range(groups):
        tall = jnp.concatenate([panel[s] for panel in panels], axis=0)
        scaled = jnp.dot(
            tall, factor[s], precision=lax.Precision.HIGHEST, preferred_element_type=jnp.float32
        )
        for d in range(deep):
            out_ref[d, s] = scaled[d * piece : (d + 1) * piece]


def multiply_tiles(deep, rows, place, *refs):
    far, slots, (out_ref, spread) = refs[:deep], refs[deep : deep + rows], refs[deep + rows :]
    groups, height, chunk = far[0].shape
    piece = slots[0].shape[2]
    for s in range(groups):
        for d in range(deep):
            slot = place[s * deep + d]
            for e in range(rows):
                first = pl.multiple_of(place[groups * deep + e] * piece, piece)
                spread[s, d, pl.ds(first, piece)] = slots[e][slot, s]
    tiles = (out_ref.shape[1] - height) // chunk
    for s in range(groups):
        wide = jnp.concatenate([piece_ref[s] for piece_ref in far], axis=1)
        tall = spread[s].reshape(deep * chunk, spread.shape[3])
        out_ref[s, :height] = jnp.dot(
            wide, tall, precision=lax.Precision.HIGHEST, preferred_element_type=jnp.float32
        )
        for t in range(tiles):
            own = spread[s, place[groups * deep + rows + t]]
            out_ref[s, height + t * chunk : height + (t + 1) * chunk] = own


def solution(mesh):
    rows, cols = mesh.shape["row"], mesh.shape["col"]
    cores, deep = 2, cols // 2
    fine = Mesh(mesh.devices.reshape(rows, deep, cores), ("row", "z", "core"))
    highest = lax.Precision.HIGHEST

    def shifted(array, axis, size, shift):
        return lax.ppermute(array, axis, [(i, (i + shift) % size) for i in range(size)])

    def gathered(array, axis, size):
        return [array] + [shifted(array, axis, size, d) for d in range(1, size)]

    def per_device(ancestor, panel, factor_inv, pattern):
        row = lax.axis_index("row")
        z = lax.axis_index("z")
        core = lax.axis_index("core")
        groups, chunk, width = panel.shape
        part = width // deep
        piece = chunk // rows
        out_rows = ancestor.shape[1] // cols
        tiles = ancestor.shape[1] // B

        def picked(slots, place, at):
            value = slots[0]
            for d in range(1, len(slots)):
                value = jnp.where((place - at) % len(slots) == d, slots[d], value)
            return value

        early = [d for d in range(1, deep) if not deep < 4 * d < 3 * deep]
        late = [d for d in range(1, deep) if d not in early]
        far = {d: shifted(ancestor, "z", deep, d) for d in early}

        whole = pl.BlockSpec(memory_space=pltpu.VMEM)
        scalars = pl.BlockSpec(memory_space=pltpu.SMEM)
        params = pltpu.CompilerParams(vmem_limit_bytes=32 * 1024 * 1024)
        quarter = (row - jnp.arange(rows, dtype=jnp.int32)) % rows

        mine = lax.dynamic_slice_in_dim(panel, row * piece, piece, axis=1)
        block = lax.dynamic_slice_in_dim(factor_inv, z * part, part, axis=2)
        panels = gathered(mine, "z", deep)
        blocks = gathered(block, "row", rows)
        scaled = pl.pallas_call(
            functools.partial(scale_pieces, deep, rows),
            out_shape=jax.ShapeDtypeStruct((deep, groups, piece, part), jnp.float32),
            in_specs=[scalars] + [whole] * (deep + rows),
            out_specs=whole,
            scratch_shapes=[pltpu.VMEM((groups, width, part), jnp.float32)],
            compiler_params=params,
        )(quarter, *panels, *blocks)
        for d in late:
            far[d] = shifted(far[d - 1], "z", deep, 1)
        slots = gathered(scaled, "row", rows)

        count = jnp.arange(deep, dtype=jnp.int32)
        at = (z - count) % deep
        stored = jnp.sum(
            jnp.where(pattern[:, :, None] == at, count[:, None], 0), axis=1, dtype=jnp.int32
        )
        from_z = ((z - stored) % deep).reshape(-1)
        own_tile = (z - row * tiles - jnp.arange(tiles, dtype=jnp.int32)) % deep
        place = jnp.concatenate([from_z, quarter, own_tile])
        height = ancestor.shape[1]
        product = pl.pallas_call(
            functools.partial(multiply_tiles, deep, rows),
            out_shape=jax.ShapeDtypeStruct((groups, height + tiles * chunk, part), jnp.float32),
            in_specs=[scalars] + [whole] * (deep + rows),
            out_specs=whole,
            scratch_shapes=[pltpu.VMEM((groups, deep, chunk, part), jnp.float32)],
            compiler_params=params,
        )(place, ancestor, *[far[d] for d in range(1, deep)], *slots)
        other = shifted(product, "core", cores, 1)

        own, own_other = [
            array[:, height:].reshape(groups, tiles, chunk, part) for array in (product, other)
        ]
        product = product[:, :height] + other[:, :height]
        halves = [jnp.where(core == 0, own, own_other), jnp.where(core == 0, own_other, own)]
        own = jnp.stack(halves, axis=2).reshape(groups, height, part)
        squares = jnp.sum(block * block, axis=1)
        term = jnp.sum(own * product, axis=1) + squares
        tail = jnp.broadcast_to(term[:, None], (groups, 8, part))

        def rows_for(c):
            block = lax.dynamic_slice_in_dim(product, (c * cores + core) * out_rows, out_rows, axis=1)
            return jnp.concatenate([block, tail], axis=1)

        moved = [rows_for(z)]
        for shift in range(1, deep):
            moved.append(shifted(rows_for((z + shift) % deep), "z", deep, shift))
        moved = jnp.concatenate([picked(moved, z, c) for c in range(deep)], axis=2)
        local = moved[:, out_rows]
        total = local
        for shift in range(1, rows):
            total = total + shifted(local, "row", rows, shift)
        return -moved[:, :out_rows], total

    col = ("z", "core")
    in_specs = (P(None, "row", col), P(None, col, None), P(None, "row", None), P())
    out_specs = (P(None, ("row", "z", "core"), None), P())
    return jax.shard_map(
        per_device, mesh=fine, in_specs=in_specs, out_specs=out_specs, check_vma=False
    )
```

```python
import functools

import jax
import jax.numpy as jnp
from jax import lax
from jax.experimental import pallas as pl
from jax.experimental.pallas import tpu as pltpu
from jax.sharding import Mesh, PartitionSpec as P

B = 256


def multiply_tiles(deep, rows, place, *refs):
    far, slots, (out_ref, spread) = refs[:deep], refs[deep : deep + rows], refs[deep + rows :]
    groups, height, chunk = far[0].shape
    piece = slots[0].shape[2]
    for s in range(groups):
        for d in range(deep):
            slot = place[s * deep + d]
            for e in range(rows):
                first = pl.multiple_of(place[groups * deep + e] * piece, piece)
                spread[s, d, pl.ds(first, piece)] = slots[e][slot, s]
    tiles = (out_ref.shape[1] - height) // chunk
    for s in range(groups):
        wide = jnp.concatenate([piece_ref[s] for piece_ref in far], axis=1)
        tall = spread[s].reshape(deep * chunk, spread.shape[3])
        out_ref[s, :height] = jnp.dot(
            wide, tall, precision=lax.Precision.HIGHEST, preferred_element_type=jnp.float32
        )
        for t in range(tiles):
            own = spread[s, place[groups * deep + rows + t]]
            out_ref[s, height + t * chunk : height + (t + 1) * chunk] = own


def solution(mesh):
    rows, cols = mesh.shape["row"], mesh.shape["col"]
    cores, deep = 2, cols // 2
    fine = Mesh(mesh.devices.reshape(rows, deep, cores), ("row", "z", "core"))
    highest = lax.Precision.HIGHEST

    def shifted(array, axis, size, shift):
        return lax.ppermute(array, axis, [(i, (i + shift) % size) for i in range(size)])

    def gathered(array, axis, size):
        return [array] + [shifted(array, axis, size, d) for d in range(1, size)]

    def per_device(ancestor, panel, factor_inv, pattern):
        row = lax.axis_index("row")
        z = lax.axis_index("z")
        core = lax.axis_index("core")
        groups, chunk, width = panel.shape
        depth = factor_inv.shape[1]
        part = width // deep
        piece = chunk // rows
        out_rows = ancestor.shape[1] // cols
        tiles = ancestor.shape[1] // B

        def picked(slots, place, at):
            value = slots[0]
            for d in range(1, len(slots)):
                value = jnp.where((place - at) % len(slots) == d, slots[d], value)
            return value

        early = [d for d in range(1, deep) if not deep < 4 * d < 3 * deep]
        late = [d for d in range(1, deep) if d not in early]
        far = {d: shifted(ancestor, "z", deep, d) for d in early}

        mine = lax.dynamic_slice_in_dim(panel, row * depth, depth, axis=2)
        partial = jnp.einsum("srw,swv->srv", mine, factor_inv, precision=highest)

        def rows_of(r):
            return lax.dynamic_slice_in_dim(partial, r * piece, piece, axis=1)

        sums = [shifted(rows_of((row + d) % rows), "row", rows, d) for d in range(1, rows)]
        squares = jnp.sum(lax.dynamic_slice_in_dim(factor_inv, z * part, part, axis=2) ** 2, axis=1)
        sums, squares = lax.optimization_barrier((sums, squares))
        scaled = sum(sums, rows_of(row))

        def columns_of(array, c):
            return lax.dynamic_slice_in_dim(array, c * part, part, axis=2)

        slots = [columns_of(scaled, z)]
        for shift in range(1, deep):
            slots.append(shifted(columns_of(scaled, (z + shift) % deep), "z", deep, shift))
        if deep > 1:
            slots, far[1] = lax.optimization_barrier((slots, far[1]))
            for d in late:
                far[d] = shifted(far[d - 1], "z", deep, 1)
        slots = gathered(jnp.stack(slots), "row", rows)

        count = jnp.arange(deep, dtype=jnp.int32)
        at = (z - count) % deep
        stored = jnp.sum(
            jnp.where(pattern[:, :, None] == at, count[:, None], 0), axis=1, dtype=jnp.int32
        )
        from_z = ((z - stored) % deep).reshape(-1)
        quarter = (row - jnp.arange(rows, dtype=jnp.int32)) % rows
        own_tile = (z - row * tiles - jnp.arange(tiles, dtype=jnp.int32)) % deep
        place = jnp.concatenate([from_z, quarter, own_tile])
        height = ancestor.shape[1]
        whole = pl.BlockSpec(memory_space=pltpu.VMEM)
        product = pl.pallas_call(
            functools.partial(multiply_tiles, deep, rows),
            out_shape=jax.ShapeDtypeStruct((groups, height + tiles * chunk, part), jnp.float32),
            in_specs=[pl.BlockSpec(memory_space=pltpu.SMEM)] + [whole] * (deep + rows),
            out_specs=whole,
            scratch_shapes=[pltpu.VMEM((groups, deep, chunk, part), jnp.float32)],
            compiler_params=pltpu.CompilerParams(vmem_limit_bytes=32 * 1024 * 1024),
        )(place, ancestor, *[far[d] for d in range(1, deep)], *slots)
        other = shifted(product, "core", cores, 1)

        own, own_other = [
            array[:, height:].reshape(groups, tiles, chunk, part) for array in (product, other)
        ]
        product = product[:, :height] + other[:, :height]
        halves = [jnp.where(core == 0, own, own_other), jnp.where(core == 0, own_other, own)]
        own = jnp.stack(halves, axis=2).reshape(groups, height, part)
        term = jnp.sum(own * product, axis=1) + squares
        tail = jnp.concatenate([term, jnp.zeros((-groups % 8, part), jnp.float32)])

        def rows_for(c):
            block = lax.dynamic_slice_in_dim(product, (c * cores + core) * out_rows, out_rows, axis=1)
            return jnp.concatenate([block.reshape(groups * out_rows, part), tail])

        moved = [rows_for(z)]
        for shift in range(1, deep):
            moved.append(shifted(rows_for((z + shift) % deep), "z", deep, shift))
        moved = jnp.concatenate([picked(moved, z, c) for c in range(deep)], axis=1)
        column_block = -moved[: groups * out_rows].reshape(groups, out_rows, width)
        total = moved[groups * out_rows : groups * out_rows + groups]
        step = 1
        while step < rows:
            total = total + lax.ppermute(total, "row", [(r, r ^ step) for r in range(rows)])
            step *= 2
        return column_block, total

    col = ("z", "core")
    in_specs = (P(None, "row", col), P(None, col, None), P(None, "row", None), P())
    out_specs = (P(None, ("row", "z", "core"), None), P())
    return jax.shard_map(
        per_device, mesh=fine, in_specs=in_specs, out_specs=out_specs, check_vma=False
    )
```

```python
import functools

import jax
import jax.numpy as jnp
from jax import lax
from jax.experimental import pallas as pl
from jax.experimental.pallas import tpu as pltpu
from jax.sharding import Mesh, PartitionSpec as P

B = 256


def multiply_tiles(deep, rows, place, *refs):
    far, slots, (out_ref, spread) = refs[:deep], refs[deep : deep + rows], refs[deep + rows :]
    groups, height, chunk = far[0].shape
    piece = slots[0].shape[2]
    for s in range(groups):
        for d in range(deep):
            slot = place[s * deep + d]
            for e in range(rows):
                first = pl.multiple_of(place[groups * deep + e] * piece, piece)
                spread[s, d, pl.ds(first, piece)] = slots[e][slot, s]
    tiles = (out_ref.shape[1] - height) // chunk
    for s in range(groups):
        wide = jnp.concatenate([piece_ref[s] for piece_ref in far], axis=1)
        tall = spread[s].reshape(deep * chunk, spread.shape[3])
        out_ref[s, :height] = jnp.dot(
            wide, tall, precision=lax.Precision.HIGHEST, preferred_element_type=jnp.float32
        )
        for t in range(tiles):
            own = spread[s, place[groups * deep + rows + t]]
            out_ref[s, height + t * chunk : height + (t + 1) * chunk] = own


def solution(mesh):
    rows, cols = mesh.shape["row"], mesh.shape["col"]
    cores, deep = 2, cols // 2
    fine = Mesh(mesh.devices.reshape(rows, deep, cores), ("row", "z", "core"))
    highest = lax.Precision.HIGHEST

    def shifted(array, axis, size, shift):
        return lax.ppermute(array, axis, [(i, (i + shift) % size) for i in range(size)])

    def gathered(array, axis, size):
        return [array] + [shifted(array, axis, size, d) for d in range(1, size)]

    def per_device(ancestor, panel, factor_inv, pattern):
        row = lax.axis_index("row")
        z = lax.axis_index("z")
        core = lax.axis_index("core")
        groups, chunk, width = panel.shape
        depth = factor_inv.shape[1]
        part = width // deep
        piece = chunk // rows
        out_rows = ancestor.shape[1] // cols
        tiles = ancestor.shape[1] // B

        def picked(slots, place, at):
            value = slots[0]
            for d in range(1, len(slots)):
                value = jnp.where((place - at) % len(slots) == d, slots[d], value)
            return value

        early = [d for d in range(1, deep) if not deep < 4 * d < 3 * deep]
        late = [d for d in range(1, deep) if d not in early]
        far = {d: shifted(ancestor, "z", deep, d) for d in early}

        mine = lax.dynamic_slice_in_dim(panel, row * depth, depth, axis=2)
        partial = jnp.einsum("srw,swv->srv", mine, factor_inv, precision=highest)

        def rows_of(r):
            return lax.dynamic_slice_in_dim(partial, r * piece, piece, axis=1)

        sums = [shifted(rows_of((row + d) % rows), "row", rows, d) for d in range(1, rows)]
        squares = jnp.sum(lax.dynamic_slice_in_dim(factor_inv, z * part, part, axis=2) ** 2, axis=1)
        sums, squares, far = lax.optimization_barrier((sums, squares, far))
        scaled = sum(sums, rows_of(row))

        def columns_of(array, c):
            return lax.dynamic_slice_in_dim(array, c * part, part, axis=2)

        slots = [columns_of(scaled, z)]
        for shift in range(1, deep):
            slots.append(shifted(columns_of(scaled, (z + shift) % deep), "z", deep, shift))
        if deep > 1:
            slots, far[1] = lax.optimization_barrier((slots, far[1]))
            for d in late:
                far[d] = shifted(far[d - 1], "z", deep, 1)
        slots = gathered(jnp.stack(slots), "row", rows)

        count = jnp.arange(deep, dtype=jnp.int32)
        at = (z - count) % deep
        stored = jnp.sum(
            jnp.where(pattern[:, :, None] == at, count[:, None], 0), axis=1, dtype=jnp.int32
        )
        from_z = ((z - stored) % deep).reshape(-1)
        quarter = (row - jnp.arange(rows, dtype=jnp.int32)) % rows
        own_tile = (z - row * tiles - jnp.arange(tiles, dtype=jnp.int32)) % deep
        place = jnp.concatenate([from_z, quarter, own_tile])
        height = ancestor.shape[1]
        whole = pl.BlockSpec(memory_space=pltpu.VMEM)
        product = pl.pallas_call(
            functools.partial(multiply_tiles, deep, rows),
            out_shape=jax.ShapeDtypeStruct((groups, height + tiles * chunk, part), jnp.float32),
            in_specs=[pl.BlockSpec(memory_space=pltpu.SMEM)] + [whole] * (deep + rows),
            out_specs=whole,
            scratch_shapes=[pltpu.VMEM((groups, deep, chunk, part), jnp.float32)],
            compiler_params=pltpu.CompilerParams(vmem_limit_bytes=32 * 1024 * 1024),
        )(place, ancestor, *[far[d] for d in range(1, deep)], *slots)
        other = shifted(product, "core", cores, 1)

        own, own_other = [
            array[:, height:].reshape(groups, tiles, chunk, part) for array in (product, other)
        ]
        product = product[:, :height] + other[:, :height]
        halves = [jnp.where(core == 0, own, own_other), jnp.where(core == 0, own_other, own)]
        own = jnp.stack(halves, axis=2).reshape(groups, height, part)
        term = jnp.sum(own * product, axis=1) + squares
        tail = jnp.concatenate([term, jnp.zeros((-groups % 8, part), jnp.float32)])

        def rows_for(c):
            block = lax.dynamic_slice_in_dim(product, (c * cores + core) * out_rows, out_rows, axis=1)
            return jnp.concatenate([block.reshape(groups * out_rows, part), tail])

        moved = [rows_for(z)]
        for shift in range(1, deep):
            moved.append(shifted(rows_for((z + shift) % deep), "z", deep, shift))
        moved = jnp.concatenate([picked(moved, z, c) for c in range(deep)], axis=1)
        column_block = -moved[: groups * out_rows].reshape(groups, out_rows, width)
        total = moved[groups * out_rows : groups * out_rows + groups]
        local = total
        for shift in range(1, rows):
            total = total + shifted(local, "row", rows, shift)
        return column_block, total

    col = ("z", "core")
    in_specs = (P(None, "row", col), P(None, col, None), P(None, "row", None), P())
    out_specs = (P(None, ("row", "z", "core"), None), P())
    return jax.shard_map(
        per_device, mesh=fine, in_specs=in_specs, out_specs=out_specs, check_vma=False
    )
```

```python
import functools

import jax
import jax.numpy as jnp
from jax import lax
from jax.experimental import pallas as pl
from jax.experimental.pallas import tpu as pltpu
from jax.sharding import Mesh, PartitionSpec as P

B = 256


def multiply_tiles(deep, rows, place, *refs):
    far, slots, (out_ref, spread) = refs[:deep], refs[deep : deep + rows], refs[deep + rows :]
    groups, height, chunk = far[0].shape
    piece = slots[0].shape[2]
    for s in range(groups):
        for d in range(deep):
            slot = place[s * deep + d]
            for e in range(rows):
                first = pl.multiple_of(place[groups * deep + e] * piece, piece)
                spread[s, d, pl.ds(first, piece)] = slots[e][slot, s]
    tiles = (out_ref.shape[1] - height) // chunk
    for s in range(groups):
        wide = jnp.concatenate([piece_ref[s] for piece_ref in far], axis=1)
        tall = spread[s].reshape(deep * chunk, spread.shape[3])
        out_ref[s, :height] = jnp.dot(
            wide, tall, precision=lax.Precision.HIGHEST, preferred_element_type=jnp.float32
        )
        for t in range(tiles):
            own = spread[s, place[groups * deep + rows + t]]
            out_ref[s, height + t * chunk : height + (t + 1) * chunk] = own


def solution(mesh):
    rows, cols = mesh.shape["row"], mesh.shape["col"]
    cores, deep = 2, cols // 2
    fine = Mesh(mesh.devices.reshape(rows, deep, cores), ("row", "z", "core"))
    highest = lax.Precision.HIGHEST

    def shifted(array, axis, size, shift):
        return lax.ppermute(array, axis, [(i, (i + shift) % size) for i in range(size)])

    def gathered(array, axis, size):
        return [array] + [shifted(array, axis, size, d) for d in range(1, size)]

    def per_device(ancestor, panel, factor_inv, pattern):
        row = lax.axis_index("row")
        z = lax.axis_index("z")
        core = lax.axis_index("core")
        groups, chunk, width = panel.shape
        depth = factor_inv.shape[1]
        part = width // deep
        piece = chunk // rows
        out_rows = ancestor.shape[1] // cols
        tiles = ancestor.shape[1] // B

        def picked(slots, place, at):
            value = slots[0]
            for d in range(1, len(slots)):
                value = jnp.where((place - at) % len(slots) == d, slots[d], value)
            return value

        early = [d for d in range(1, deep) if not deep < 4 * d < 3 * deep]
        late = [d for d in range(1, deep) if d not in early]
        far = {d: shifted(ancestor, "z", deep, d) for d in early[:1]}

        mine = lax.dynamic_slice_in_dim(panel, row * depth, depth, axis=2)
        partial = jnp.einsum("srw,swv->srv", mine, factor_inv, precision=highest)
        partial, held_back = lax.optimization_barrier((partial, ancestor))
        far |= {d: shifted(held_back, "z", deep, d) for d in early[1:]}

        def rows_of(r):
            return lax.dynamic_slice_in_dim(partial, r * piece, piece, axis=1)

        sums = [shifted(rows_of((row + d) % rows), "row", rows, d) for d in range(1, rows)]
        squares = jnp.sum(lax.dynamic_slice_in_dim(factor_inv, z * part, part, axis=2) ** 2, axis=1)
        sums, squares = lax.optimization_barrier((sums, squares))
        scaled = sum(sums, rows_of(row))

        def columns_of(array, c):
            return lax.dynamic_slice_in_dim(array, c * part, part, axis=2)

        slots = [columns_of(scaled, z)]
        for shift in range(1, deep):
            slots.append(shifted(columns_of(scaled, (z + shift) % deep), "z", deep, shift))
        if deep > 1:
            slots, far[1] = lax.optimization_barrier((slots, far[1]))
            for d in late:
                far[d] = shifted(far[d - 1], "z", deep, 1)
        slots = gathered(jnp.stack(slots), "row", rows)

        count = jnp.arange(deep, dtype=jnp.int32)
        at = (z - count) % deep
        stored = jnp.sum(
            jnp.where(pattern[:, :, None] == at, count[:, None], 0), axis=1, dtype=jnp.int32
        )
        from_z = ((z - stored) % deep).reshape(-1)
        quarter = (row - jnp.arange(rows, dtype=jnp.int32)) % rows
        own_tile = (z - row * tiles - jnp.arange(tiles, dtype=jnp.int32)) % deep
        place = jnp.concatenate([from_z, quarter, own_tile])
        height = ancestor.shape[1]
        whole = pl.BlockSpec(memory_space=pltpu.VMEM)
        product = pl.pallas_call(
            functools.partial(multiply_tiles, deep, rows),
            out_shape=jax.ShapeDtypeStruct((groups, height + tiles * chunk, part), jnp.float32),
            in_specs=[pl.BlockSpec(memory_space=pltpu.SMEM)] + [whole] * (deep + rows),
            out_specs=whole,
            scratch_shapes=[pltpu.VMEM((groups, deep, chunk, part), jnp.float32)],
            compiler_params=pltpu.CompilerParams(vmem_limit_bytes=32 * 1024 * 1024),
        )(place, ancestor, *[far[d] for d in range(1, deep)], *slots)
        other = shifted(product, "core", cores, 1)

        own, own_other = [
            array[:, height:].reshape(groups, tiles, chunk, part) for array in (product, other)
        ]
        product = product[:, :height] + other[:, :height]
        halves = [jnp.where(core == 0, own, own_other), jnp.where(core == 0, own_other, own)]
        own = jnp.stack(halves, axis=2).reshape(groups, height, part)
        term = jnp.sum(own * product, axis=1) + squares
        tail = jnp.concatenate([term, jnp.zeros((-groups % 8, part), jnp.float32)])

        def rows_for(c):
            block = lax.dynamic_slice_in_dim(product, (c * cores + core) * out_rows, out_rows, axis=1)
            return jnp.concatenate([block.reshape(groups * out_rows, part), tail])

        moved = [rows_for(z)]
        for shift in range(1, deep):
            moved.append(shifted(rows_for((z + shift) % deep), "z", deep, shift))
        moved = jnp.concatenate([picked(moved, z, c) for c in range(deep)], axis=1)
        column_block = -moved[: groups * out_rows].reshape(groups, out_rows, width)
        total = moved[groups * out_rows : groups * out_rows + groups]
        local = total
        for shift in range(1, rows):
            total = total + shifted(local, "row", rows, shift)
        return column_block, total

    col = ("z", "core")
    in_specs = (P(None, "row", col), P(None, col, None), P(None, "row", None), P())
    out_specs = (P(None, ("row", "z", "core"), None), P())
    return jax.shard_map(
        per_device, mesh=fine, in_specs=in_specs, out_specs=out_specs, check_vma=False
    )
```

```python
import functools

import jax
import jax.numpy as jnp
from jax import lax
from jax.experimental import pallas as pl
from jax.experimental.pallas import tpu as pltpu
from jax.sharding import Mesh, PartitionSpec as P

B = 256


def multiply_tiles(deep, rows, place, *refs):
    far, slots, (out_ref, spread) = refs[:deep], refs[deep : deep + rows], refs[deep + rows :]
    groups, height, chunk = far[0].shape
    piece = slots[0].shape[2]
    for s in range(groups):
        for d in range(deep):
            slot = place[s * deep + d]
            for e in range(rows):
                first = pl.multiple_of(place[groups * deep + e] * piece, piece)
                spread[s, d, pl.ds(first, piece)] = slots[e][slot, s]
    tiles = (out_ref.shape[1] - height) // chunk
    for s in range(groups):
        wide = jnp.concatenate([piece_ref[s] for piece_ref in far], axis=1)
        tall = spread[s].reshape(deep * chunk, spread.shape[3])
        out_ref[s, :height] = jnp.dot(
            wide, tall, precision=lax.Precision.HIGHEST, preferred_element_type=jnp.float32
        )
        for t in range(tiles):
            own = spread[s, place[groups * deep + rows + t]]
            out_ref[s, height + t * chunk : height + (t + 1) * chunk] = own


def solution(mesh):
    rows, cols = mesh.shape["row"], mesh.shape["col"]
    cores, deep = 2, cols // 2
    fine = Mesh(mesh.devices.reshape(rows, deep, cores), ("row", "z", "core"))
    highest = lax.Precision.HIGHEST

    def shifted(array, axis, size, shift):
        return lax.ppermute(array, axis, [(i, (i + shift) % size) for i in range(size)])

    def gathered(array, axis, size):
        return [array] + [shifted(array, axis, size, d) for d in range(1, size)]

    def per_device(ancestor, panel, factor_inv, pattern):
        row = lax.axis_index("row")
        z = lax.axis_index("z")
        core = lax.axis_index("core")
        groups, chunk, width = panel.shape
        depth = factor_inv.shape[1]
        part = width // deep
        piece = chunk // rows
        out_rows = ancestor.shape[1] // cols
        tiles = ancestor.shape[1] // B

        def picked(slots, place, at):
            value = slots[0]
            for d in range(1, len(slots)):
                value = jnp.where((place - at) % len(slots) == d, slots[d], value)
            return value

        early = [d for d in range(1, deep) if not deep < 4 * d < 3 * deep]
        late = [d for d in range(1, deep) if d not in early]
        far = {d: shifted(ancestor, "z", deep, d) for d in early[:1]}

        mine = lax.dynamic_slice_in_dim(panel, row * depth, depth, axis=2)
        partial = jnp.einsum("srw,swv->srv", mine, factor_inv, precision=highest)
        partial, held_back = lax.optimization_barrier((partial, ancestor))
        far |= {d: shifted(held_back, "z", deep, d) for d in early[1:]}

        def rows_of(r):
            return lax.dynamic_slice_in_dim(partial, r * piece, piece, axis=1)

        sums = [shifted(rows_of((row + d) % rows), "row", rows, d) for d in range(1, rows)]
        squares = jnp.sum(lax.dynamic_slice_in_dim(factor_inv, z * part, part, axis=2) ** 2, axis=1)
        sums, squares = lax.optimization_barrier((sums, squares))
        scaled = sum(sums, rows_of(row))

        def columns_of(array, c):
            return lax.dynamic_slice_in_dim(array, c * part, part, axis=2)

        slots = [columns_of(scaled, z)]
        for shift in range(1, deep):
            slots.append(shifted(columns_of(scaled, (z + shift) % deep), "z", deep, shift))
        if deep > 1:
            for d in reversed(late):
                far[d] = shifted(far[d + 1], "z", deep, deep - 1)
        slots = gathered(jnp.stack(slots), "row", rows)

        count = jnp.arange(deep, dtype=jnp.int32)
        at = (z - count) % deep
        stored = jnp.sum(
            jnp.where(pattern[:, :, None] == at, count[:, None], 0), axis=1, dtype=jnp.int32
        )
        from_z = ((z - stored) % deep).reshape(-1)
        quarter = (row - jnp.arange(rows, dtype=jnp.int32)) % rows
        own_tile = (z - row * tiles - jnp.arange(tiles, dtype=jnp.int32)) % deep
        place = jnp.concatenate([from_z, quarter, own_tile])
        height = ancestor.shape[1]
        whole = pl.BlockSpec(memory_space=pltpu.VMEM)
        product = pl.pallas_call(
            functools.partial(multiply_tiles, deep, rows),
            out_shape=jax.ShapeDtypeStruct((groups, height + tiles * chunk, part), jnp.float32),
            in_specs=[pl.BlockSpec(memory_space=pltpu.SMEM)] + [whole] * (deep + rows),
            out_specs=whole,
            scratch_shapes=[pltpu.VMEM((groups, deep, chunk, part), jnp.float32)],
            compiler_params=pltpu.CompilerParams(vmem_limit_bytes=32 * 1024 * 1024),
        )(place, ancestor, *[far[d] for d in range(1, deep)], *slots)
        other = shifted(product, "core", cores, 1)

        own, own_other = [
            array[:, height:].reshape(groups, tiles, chunk, part) for array in (product, other)
        ]
        product = product[:, :height] + other[:, :height]
        halves = [jnp.where(core == 0, own, own_other), jnp.where(core == 0, own_other, own)]
        own = jnp.stack(halves, axis=2).reshape(groups, height, part)
        term = jnp.sum(own * product, axis=1) + squares
        tail = jnp.concatenate([term, jnp.zeros((-groups % 8, part), jnp.float32)])

        def rows_for(c):
            block = lax.dynamic_slice_in_dim(product, (c * cores + core) * out_rows, out_rows, axis=1)
            return jnp.concatenate([block.reshape(groups * out_rows, part), tail])

        moved = [rows_for(z)]
        for shift in range(1, deep):
            moved.append(shifted(rows_for((z + shift) % deep), "z", deep, shift))
        moved = jnp.concatenate([picked(moved, z, c) for c in range(deep)], axis=1)
        column_block = -moved[: groups * out_rows].reshape(groups, out_rows, width)
        total = moved[groups * out_rows : groups * out_rows + groups]
        local = total
        for shift in range(1, rows):
            total = total + shifted(local, "row", rows, shift)
        return column_block, total

    col = ("z", "core")
    in_specs = (P(None, "row", col), P(None, col, None), P(None, "row", None), P())
    out_specs = (P(None, ("row", "z", "core"), None), P())
    return jax.shard_map(
        per_device, mesh=fine, in_specs=in_specs, out_specs=out_specs, check_vma=False
    )
```

```python
import functools

import jax
import jax.numpy as jnp
from jax import lax
from jax.experimental import pallas as pl
from jax.experimental.pallas import tpu as pltpu
from jax.sharding import Mesh, PartitionSpec as P

B = 256


def multiply_tiles(deep, rows, place, *refs):
    far, slots, (out_ref, spread) = refs[:deep], refs[deep : deep + rows], refs[deep + rows :]
    groups, height, chunk = far[0].shape
    piece = slots[0].shape[2]
    for s in range(groups):
        for d in range(deep):
            slot = place[s * deep + d]
            for e in range(rows):
                first = pl.multiple_of(place[groups * deep + e] * piece, piece)
                spread[s, d, pl.ds(first, piece)] = slots[e][slot, s]
    tiles = (out_ref.shape[1] - height) // chunk
    for s in range(groups):
        wide = jnp.concatenate([piece_ref[s] for piece_ref in far], axis=1)
        tall = spread[s].reshape(deep * chunk, spread.shape[3])
        out_ref[s, :height] = jnp.dot(
            wide, tall, precision=lax.Precision.HIGHEST, preferred_element_type=jnp.float32
        )
        for t in range(tiles):
            own = spread[s, place[groups * deep + rows + t]]
            out_ref[s, height + t * chunk : height + (t + 1) * chunk] = own


def solution(mesh):
    rows, cols = mesh.shape["row"], mesh.shape["col"]
    cores, deep = 2, cols // 2
    fine = Mesh(mesh.devices.reshape(rows, deep, cores), ("row", "z", "core"))
    highest = lax.Precision.HIGHEST

    def shifted(array, axis, size, shift):
        return lax.ppermute(array, axis, [(i, (i + shift) % size) for i in range(size)])

    def traded(array, axis, size, other):
        return lax.ppermute(array, axis, [(i, i ^ other) for i in range(size)])

    def gathered(array, axis, size):
        return [array] + [traded(array, axis, size, d) for d in range(1, size)]

    def per_device(ancestor, panel, factor_inv, pattern):
        row = lax.axis_index("row")
        z = lax.axis_index("z")
        core = lax.axis_index("core")
        groups, chunk, width = panel.shape
        depth = factor_inv.shape[1]
        part = width // deep
        piece = chunk // rows
        out_rows = ancestor.shape[1] // cols
        tiles = ancestor.shape[1] // B

        def picked(slots, place, at):
            value = slots[0]
            for d in range(1, len(slots)):
                value = jnp.where(place ^ at == d, slots[d], value)
            return value

        early = [d for d in range(1, deep) if not deep < 4 * d < 3 * deep]
        late = [d for d in range(1, deep) if d not in early]
        far = {d: shifted(ancestor, "z", deep, d) for d in early[:1]}

        mine = lax.dynamic_slice_in_dim(panel, row * depth, depth, axis=2)
        partial = jnp.einsum("srw,swv->srv", mine, factor_inv, precision=highest)
        partial, held_back = lax.optimization_barrier((partial, ancestor))
        far |= {d: shifted(held_back, "z", deep, d) for d in early[1:]}

        def rows_of(r):
            return lax.dynamic_slice_in_dim(partial, r * piece, piece, axis=1)

        sums = [traded(rows_of(row ^ d), "row", rows, d) for d in range(1, rows)]
        squares = jnp.sum(lax.dynamic_slice_in_dim(factor_inv, z * part, part, axis=2) ** 2, axis=1)
        sums, squares = lax.optimization_barrier((sums, squares))
        scaled = sum(sums, rows_of(row))

        def columns_of(array, c):
            return lax.dynamic_slice_in_dim(array, c * part, part, axis=2)

        slots = [columns_of(scaled, z)]
        for d in range(1, deep):
            slots.append(traded(columns_of(scaled, z ^ d), "z", deep, d))
        if deep > 1:
            for d in reversed(late):
                far[d] = shifted(far[d + 1], "z", deep, deep - 1)
        slots = gathered(jnp.stack(slots), "row", rows)

        count = jnp.arange(deep, dtype=jnp.int32)
        at = (z - count) % deep
        stored = jnp.sum(
            jnp.where(pattern[:, :, None] == at, count[:, None], 0), axis=1, dtype=jnp.int32
        )
        from_z = (z ^ stored).reshape(-1)
        quarter = row ^ jnp.arange(rows, dtype=jnp.int32)
        own_tile = (z - row * tiles - jnp.arange(tiles, dtype=jnp.int32)) % deep
        place = jnp.concatenate([from_z, quarter, own_tile])
        height = ancestor.shape[1]
        whole = pl.BlockSpec(memory_space=pltpu.VMEM)
        product = pl.pallas_call(
            functools.partial(multiply_tiles, deep, rows),
            out_shape=jax.ShapeDtypeStruct((groups, height + tiles * chunk, part), jnp.float32),
            in_specs=[pl.BlockSpec(memory_space=pltpu.SMEM)] + [whole] * (deep + rows),
            out_specs=whole,
            scratch_shapes=[pltpu.VMEM((groups, deep, chunk, part), jnp.float32)],
            compiler_params=pltpu.CompilerParams(vmem_limit_bytes=32 * 1024 * 1024),
        )(place, ancestor, *[far[d] for d in range(1, deep)], *slots)
        other = shifted(product, "core", cores, 1)

        own, own_other = [
            array[:, height:].reshape(groups, tiles, chunk, part) for array in (product, other)
        ]
        product = product[:, :height] + other[:, :height]
        halves = [jnp.where(core == 0, own, own_other), jnp.where(core == 0, own_other, own)]
        own = jnp.stack(halves, axis=2).reshape(groups, height, part)
        term = jnp.sum(own * product, axis=1) + squares
        tail = jnp.concatenate([term, jnp.zeros((-groups % 8, part), jnp.float32)])

        def rows_for(c):
            block = lax.dynamic_slice_in_dim(product, (c * cores + core) * out_rows, out_rows, axis=1)
            return jnp.concatenate([block.reshape(groups * out_rows, part), tail])

        moved = [rows_for(z)]
        for d in range(1, deep):
            moved.append(traded(rows_for(z ^ d), "z", deep, d))
        moved = jnp.concatenate([picked(moved, z, c) for c in range(deep)], axis=1)
        column_block = -moved[: groups * out_rows].reshape(groups, out_rows, width)
        total = moved[groups * out_rows : groups * out_rows + groups]
        local = total
        for d in range(1, rows):
            total = total + traded(local, "row", rows, d)
        return column_block, total

    col = ("z", "core")
    in_specs = (P(None, "row", col), P(None, col, None), P(None, "row", None), P())
    out_specs = (P(None, ("row", "z", "core"), None), P())
    return jax.shard_map(
        per_device, mesh=fine, in_specs=in_specs, out_specs=out_specs, check_vma=False
    )
```

```python
import functools

import jax
import jax.numpy as jnp
from jax import lax
from jax.experimental import pallas as pl
from jax.experimental.pallas import tpu as pltpu
from jax.sharding import Mesh, PartitionSpec as P

B = 256


def multiply_tiles(deep, rows, place, *refs):
    far, slots, (out_ref, spread) = refs[:deep], refs[deep : deep + rows], refs[deep + rows :]
    groups, height, chunk = far[0].shape
    piece = slots[0].shape[2]
    for s in range(groups):
        for d in range(deep):
            slot = place[s * deep + d]
            for e in range(rows):
                first = pl.multiple_of(place[groups * deep + e] * piece, piece)
                spread[s, d, pl.ds(first, piece)] = slots[e][slot, s]
    tiles = (out_ref.shape[1] - height) // chunk
    for s in range(groups):
        wide = jnp.concatenate([piece_ref[s] for piece_ref in far], axis=1)
        tall = spread[s].reshape(deep * chunk, spread.shape[3])
        out_ref[s, :height] = jnp.dot(
            wide, tall, precision=lax.Precision.HIGHEST, preferred_element_type=jnp.float32
        )
        for t in range(tiles):
            own = spread[s, place[groups * deep + rows + t]]
            out_ref[s, height + t * chunk : height + (t + 1) * chunk] = own


def solution(mesh):
    rows, cols = mesh.shape["row"], mesh.shape["col"]
    cores, deep = 2, cols // 2
    fine = Mesh(mesh.devices.reshape(rows, deep, cores), ("row", "z", "core"))
    highest = lax.Precision.HIGHEST

    def shifted(array, axis, size, shift):
        return lax.ppermute(array, axis, [(i, (i + shift) % size) for i in range(size)])

    def traded(array, axis, size, other):
        return lax.ppermute(array, axis, [(i, i ^ other) for i in range(size)])

    def gathered(array, axis, size):
        return [array] + [traded(array, axis, size, d) for d in reversed(range(1, size))][::-1]

    def per_device(ancestor, panel, factor_inv, pattern):
        row = lax.axis_index("row")
        z = lax.axis_index("z")
        core = lax.axis_index("core")
        groups, chunk, width = panel.shape
        depth = factor_inv.shape[1]
        part = width // deep
        piece = chunk // rows
        out_rows = ancestor.shape[1] // cols
        tiles = ancestor.shape[1] // B

        def picked(slots, place, at):
            value = slots[0]
            for d in range(1, len(slots)):
                value = jnp.where(place ^ at == d, slots[d], value)
            return value

        early = [d for d in range(1, deep) if not deep < 4 * d < 3 * deep]
        late = [d for d in range(1, deep) if d not in early]
        far = {d: shifted(ancestor, "z", deep, d) for d in early[:1]}

        mine = lax.dynamic_slice_in_dim(panel, row * depth, depth, axis=2)
        partial = jnp.einsum("srw,swv->srv", mine, factor_inv, precision=highest)
        partial, held_back = lax.optimization_barrier((partial, ancestor))
        far |= {d: shifted(held_back, "z", deep, d) for d in early[1:]}

        def rows_of(r):
            return lax.dynamic_slice_in_dim(partial, r * piece, piece, axis=1)

        sums = [traded(rows_of(row ^ d), "row", rows, d) for d in reversed(range(1, rows))]
        squares = jnp.sum(lax.dynamic_slice_in_dim(factor_inv, z * part, part, axis=2) ** 2, axis=1)
        sums, squares = lax.optimization_barrier((sums, squares))
        scaled = sum(sums, rows_of(row))

        def columns_of(array, c):
            return lax.dynamic_slice_in_dim(array, c * part, part, axis=2)

        slots = [traded(columns_of(scaled, z ^ d), "z", deep, d) for d in reversed(range(1, deep))]
        slots = [columns_of(scaled, z)] + slots[::-1]
        if deep > 1:
            for d in reversed(late):
                far[d] = shifted(far[d + 1], "z", deep, deep - 1)
        slots = gathered(jnp.stack(slots), "row", rows)

        count = jnp.arange(deep, dtype=jnp.int32)
        at = (z - count) % deep
        stored = jnp.sum(
            jnp.where(pattern[:, :, None] == at, count[:, None], 0), axis=1, dtype=jnp.int32
        )
        from_z = (z ^ stored).reshape(-1)
        quarter = row ^ jnp.arange(rows, dtype=jnp.int32)
        own_tile = (z - row * tiles - jnp.arange(tiles, dtype=jnp.int32)) % deep
        place = jnp.concatenate([from_z, quarter, own_tile])
        height = ancestor.shape[1]
        whole = pl.BlockSpec(memory_space=pltpu.VMEM)
        product = pl.pallas_call(
            functools.partial(multiply_tiles, deep, rows),
            out_shape=jax.ShapeDtypeStruct((groups, height + tiles * chunk, part), jnp.float32),
            in_specs=[pl.BlockSpec(memory_space=pltpu.SMEM)] + [whole] * (deep + rows),
            out_specs=whole,
            scratch_shapes=[pltpu.VMEM((groups, deep, chunk, part), jnp.float32)],
            compiler_params=pltpu.CompilerParams(vmem_limit_bytes=32 * 1024 * 1024),
        )(place, ancestor, *[far[d] for d in range(1, deep)], *slots)
        other = shifted(product, "core", cores, 1)

        own, own_other = [
            array[:, height:].reshape(groups, tiles, chunk, part) for array in (product, other)
        ]
        product = product[:, :height] + other[:, :height]
        halves = [jnp.where(core == 0, own, own_other), jnp.where(core == 0, own_other, own)]
        own = jnp.stack(halves, axis=2).reshape(groups, height, part)
        term = jnp.sum(own * product, axis=1) + squares
        tail = jnp.concatenate([term, jnp.zeros((-groups % 8, part), jnp.float32)])

        def rows_for(c):
            block = lax.dynamic_slice_in_dim(product, (c * cores + core) * out_rows, out_rows, axis=1)
            return jnp.concatenate([block.reshape(groups * out_rows, part), tail])

        moved = [traded(rows_for(z ^ d), "z", deep, d) for d in reversed(range(1, deep))]
        moved = [rows_for(z)] + moved[::-1]
        moved = jnp.concatenate([picked(moved, z, c) for c in range(deep)], axis=1)
        column_block = -moved[: groups * out_rows].reshape(groups, out_rows, width)
        total = moved[groups * out_rows : groups * out_rows + groups]
        local = total
        for d in reversed(range(1, rows)):
            total = total + traded(local, "row", rows, d)
        return column_block, total

    col = ("z", "core")
    in_specs = (P(None, "row", col), P(None, col, None), P(None, "row", None), P())
    out_specs = (P(None, ("row", "z", "core"), None), P())
    return jax.shard_map(
        per_device, mesh=fine, in_specs=in_specs, out_specs=out_specs, check_vma=False
    )
```

```python
import functools

import jax
import jax.numpy as jnp
from jax import lax
from jax.experimental import pallas as pl
from jax.experimental.pallas import tpu as pltpu
from jax.sharding import Mesh, PartitionSpec as P

B = 256


def multiply_tiles(deep, rows, place, *refs):
    far, slots, (out_ref, spread) = refs[:deep], refs[deep : deep + rows], refs[deep + rows :]
    groups, height, chunk = far[0].shape
    piece = slots[0].shape[2]
    for s in range(groups):
        for d in range(deep):
            slot = place[s * deep + d]
            for e in range(rows):
                first = pl.multiple_of(place[groups * deep + e] * piece, piece)
                spread[s, d, pl.ds(first, piece)] = slots[e][slot, s]
    tiles = (out_ref.shape[1] - height) // chunk
    for s in range(groups):
        wide = jnp.concatenate([piece_ref[s] for piece_ref in far], axis=1)
        tall = spread[s].reshape(deep * chunk, spread.shape[3])
        out_ref[s, :height] = jnp.dot(
            wide, tall, precision=lax.Precision.HIGHEST, preferred_element_type=jnp.float32
        )
        for t in range(tiles):
            own = spread[s, place[groups * deep + rows + t]]
            out_ref[s, height + t * chunk : height + (t + 1) * chunk] = own


def solution(mesh):
    rows, cols = mesh.shape["row"], mesh.shape["col"]
    cores, deep = 2, cols // 2
    fine = Mesh(mesh.devices.reshape(rows, deep, cores), ("row", "z", "core"))
    highest = lax.Precision.HIGHEST

    def traded(array, axis, size, other):
        return lax.ppermute(array, axis, [(i, i ^ other) for i in range(size)])

    def gathered(array, axis, size):
        return [array] + [traded(array, axis, size, d) for d in reversed(range(1, size))][::-1]

    def per_device(ancestor, panel, factor_inv, pattern):
        row = lax.axis_index("row")
        z = lax.axis_index("z")
        core = lax.axis_index("core")
        groups, chunk, width = panel.shape
        depth = factor_inv.shape[1]
        part = width // deep
        piece = chunk // rows
        out_rows = ancestor.shape[1] // cols
        tiles = ancestor.shape[1] // B

        def picked(slots, place, at):
            value = slots[0]
            for d in range(1, len(slots)):
                value = jnp.where(place ^ at == d, slots[d], value)
            return value

        far = {d: traded(ancestor, "z", deep, d) for d in range(2, deep, 2)}

        mine = lax.dynamic_slice_in_dim(panel, row * depth, depth, axis=2)
        partial = jnp.einsum("srw,swv->srv", mine, factor_inv, precision=highest)
        partial, held_back = lax.optimization_barrier((partial, ancestor))
        far |= {d: traded(held_back, "z", deep, d) for d in range(1, min(deep, 2))}

        def rows_of(r):
            return lax.dynamic_slice_in_dim(partial, r * piece, piece, axis=1)

        sums = [traded(rows_of(row ^ d), "row", rows, d) for d in reversed(range(1, rows))]
        squares = jnp.sum(lax.dynamic_slice_in_dim(factor_inv, z * part, part, axis=2) ** 2, axis=1)
        sums, squares = lax.optimization_barrier((sums, squares))
        scaled = sum(sums, rows_of(row))

        def columns_of(array, c):
            return lax.dynamic_slice_in_dim(array, c * part, part, axis=2)

        slots = [traded(columns_of(scaled, z ^ d), "z", deep, d) for d in reversed(range(1, deep))]
        slots = [columns_of(scaled, z)] + slots[::-1]
        far |= {d: traded(far[d - 1], "z", deep, 1) for d in range(3, deep, 2)}
        slots = gathered(jnp.stack(slots), "row", rows)

        count = jnp.arange(deep, dtype=jnp.int32)
        at = z ^ count
        stored = jnp.sum(
            jnp.where(pattern[:, :, None] == at, count[:, None], 0), axis=1, dtype=jnp.int32
        )
        from_z = (z ^ stored).reshape(-1)
        quarter = row ^ jnp.arange(rows, dtype=jnp.int32)
        own_tile = z ^ (row * tiles + jnp.arange(tiles, dtype=jnp.int32))
        place = jnp.concatenate([from_z, quarter, own_tile])
        height = ancestor.shape[1]
        whole = pl.BlockSpec(memory_space=pltpu.VMEM)
        product = pl.pallas_call(
            functools.partial(multiply_tiles, deep, rows),
            out_shape=jax.ShapeDtypeStruct((groups, height + tiles * chunk, part), jnp.float32),
            in_specs=[pl.BlockSpec(memory_space=pltpu.SMEM)] + [whole] * (deep + rows),
            out_specs=whole,
            scratch_shapes=[pltpu.VMEM((groups, deep, chunk, part), jnp.float32)],
            compiler_params=pltpu.CompilerParams(vmem_limit_bytes=32 * 1024 * 1024),
        )(place, ancestor, *[far[d] for d in range(1, deep)], *slots)
        other = traded(product, "core", cores, 1)

        own, own_other = [
            array[:, height:].reshape(groups, tiles, chunk, part) for array in (product, other)
        ]
        product = product[:, :height] + other[:, :height]
        halves = [jnp.where(core == 0, own, own_other), jnp.where(core == 0, own_other, own)]
        own = jnp.stack(halves, axis=2).reshape(groups, height, part)
        term = jnp.sum(own * product, axis=1) + squares
        tail = jnp.concatenate([term, jnp.zeros((-groups % 8, part), jnp.float32)])

        def rows_for(c):
            block = lax.dynamic_slice_in_dim(product, (c * cores + core) * out_rows, out_rows, axis=1)
            return jnp.concatenate([block.reshape(groups * out_rows, part), tail])

        moved = [traded(rows_for(z ^ d), "z", deep, d) for d in reversed(range(1, deep))]
        moved = [rows_for(z)] + moved[::-1]
        moved = jnp.concatenate([picked(moved, z, c) for c in range(deep)], axis=1)
        column_block = -moved[: groups * out_rows].reshape(groups, out_rows, width)
        total = moved[groups * out_rows : groups * out_rows + groups]
        local = total
        for d in reversed(range(1, rows)):
            total = total + traded(local, "row", rows, d)
        return column_block, total

    col = ("z", "core")
    in_specs = (P(None, "row", col), P(None, col, None), P(None, "row", None), P())
    out_specs = (P(None, ("row", "z", "core"), None), P())
    return jax.shard_map(
        per_device, mesh=fine, in_specs=in_specs, out_specs=out_specs, check_vma=False
    )
```

```python
import functools

import jax
import jax.numpy as jnp
from jax import lax
from jax.experimental import pallas as pl
from jax.experimental.pallas import tpu as pltpu
from jax.sharding import Mesh, PartitionSpec as P

B = 256


def multiply_tiles(deep, rows, place, *refs):
    far, slots, (out_ref, spread) = refs[:deep], refs[deep : deep + rows], refs[deep + rows :]
    groups, height, chunk = far[0].shape
    piece = slots[0].shape[2]
    for s in range(groups):
        for d in range(deep):
            slot = place[s * deep + d]
            for e in range(rows):
                first = pl.multiple_of(place[groups * deep + e] * piece, piece)
                spread[s, d, pl.ds(first, piece)] = slots[e][slot, s]
    tiles = (out_ref.shape[1] - height) // chunk
    for s in range(groups):
        wide = jnp.concatenate([piece_ref[s] for piece_ref in far], axis=1)
        tall = spread[s].reshape(deep * chunk, spread.shape[3])
        out_ref[s, :height] = jnp.dot(
            wide, tall, precision=lax.Precision.HIGH, preferred_element_type=jnp.float32
        )
        for t in range(tiles):
            own = spread[s, place[groups * deep + rows + t]]
            out_ref[s, height + t * chunk : height + (t + 1) * chunk] = own


def solution(mesh):
    rows, cols = mesh.shape["row"], mesh.shape["col"]
    cores, deep = 2, cols // 2
    fine = Mesh(mesh.devices.reshape(rows, deep, cores), ("row", "z", "core"))
    high = lax.Precision.HIGH

    def shifted(array, axis, size, shift):
        return lax.ppermute(array, axis, [(i, (i + shift) % size) for i in range(size)])

    def traded(array, axis, size, other):
        return lax.ppermute(array, axis, [(i, i ^ other) for i in range(size)])

    def gathered(array, axis, size):
        return [array] + [traded(array, axis, size, d) for d in range(1, size)]

    def per_device(ancestor, panel, factor_inv, pattern):
        row = lax.axis_index("row")
        z = lax.axis_index("z")
        core = lax.axis_index("core")
        groups, chunk, width = panel.shape
        depth = factor_inv.shape[1]
        part = width // deep
        piece = chunk // rows
        out_rows = ancestor.shape[1] // cols
        tiles = ancestor.shape[1] // B

        def picked(slots, place, at):
            value = slots[0]
            for d in range(1, len(slots)):
                value = jnp.where(place ^ at == d, slots[d], value)
            return value

        early = [d for d in range(1, deep) if not deep < 4 * d < 3 * deep]
        late = [d for d in range(1, deep) if d not in early]
        far = {d: shifted(ancestor, "z", deep, d) for d in early[:1]}

        mine = lax.dynamic_slice_in_dim(panel, row * depth, depth, axis=2)
        partial = jnp.einsum("srw,swv->srv", mine, factor_inv, precision=high)
        partial, held_back = lax.optimization_barrier((partial, ancestor))
        far |= {d: shifted(held_back, "z", deep, d) for d in early[1:]}

        def rows_of(r):
            return lax.dynamic_slice_in_dim(partial, r * piece, piece, axis=1)

        sums = [traded(rows_of(row ^ d), "row", rows, d) for d in range(1, rows)]
        squares = jnp.sum(lax.dynamic_slice_in_dim(factor_inv, z * part, part, axis=2) ** 2, axis=1)
        sums, squares = lax.optimization_barrier((sums, squares))
        scaled = sum(sums, rows_of(row))

        def columns_of(array, c):
            return lax.dynamic_slice_in_dim(array, c * part, part, axis=2)

        slots = [columns_of(scaled, z)]
        for d in range(1, deep):
            slots.append(traded(columns_of(scaled, z ^ d), "z", deep, d))
        if deep > 1:
            for d in reversed(late):
                far[d] = shifted(far[d + 1], "z", deep, deep - 1)
        slots = gathered(jnp.stack(slots), "row", rows)

        count = jnp.arange(deep, dtype=jnp.int32)
        at = (z - count) % deep
        stored = jnp.sum(
            jnp.where(pattern[:, :, None] == at, count[:, None], 0), axis=1, dtype=jnp.int32
        )
        from_z = (z ^ stored).reshape(-1)
        quarter = row ^ jnp.arange(rows, dtype=jnp.int32)
        own_tile = (z - row * tiles - jnp.arange(tiles, dtype=jnp.int32)) % deep
        place = jnp.concatenate([from_z, quarter, own_tile])
        height = ancestor.shape[1]
        whole = pl.BlockSpec(memory_space=pltpu.VMEM)
        product = pl.pallas_call(
            functools.partial(multiply_tiles, deep, rows),
            out_shape=jax.ShapeDtypeStruct((groups, height + tiles * chunk, part), jnp.float32),
            in_specs=[pl.BlockSpec(memory_space=pltpu.SMEM)] + [whole] * (deep + rows),
            out_specs=whole,
            scratch_shapes=[pltpu.VMEM((groups, deep, chunk, part), jnp.float32)],
            compiler_params=pltpu.CompilerParams(vmem_limit_bytes=32 * 1024 * 1024),
        )(place, ancestor, *[far[d] for d in range(1, deep)], *slots)
        other = shifted(product, "core", cores, 1)

        own, own_other = [
            array[:, height:].reshape(groups, tiles, chunk, part) for array in (product, other)
        ]
        product = product[:, :height] + other[:, :height]
        halves = [jnp.where(core == 0, own, own_other), jnp.where(core == 0, own_other, own)]
        own = jnp.stack(halves, axis=2).reshape(groups, height, part)
        term = jnp.sum(own * product, axis=1) + squares
        tail = jnp.concatenate([term, jnp.zeros((-groups % 8, part), jnp.float32)])

        def rows_for(c):
            block = lax.dynamic_slice_in_dim(product, (c * cores + core) * out_rows, out_rows, axis=1)
            return jnp.concatenate([block.reshape(groups * out_rows, part), tail])

        moved = [rows_for(z)]
        for d in range(1, deep):
            moved.append(traded(rows_for(z ^ d), "z", deep, d))
        moved = jnp.concatenate([picked(moved, z, c) for c in range(deep)], axis=1)
        column_block = -moved[: groups * out_rows].reshape(groups, out_rows, width)
        total = moved[groups * out_rows : groups * out_rows + groups]
        local = total
        for d in range(1, rows):
            total = total + traded(local, "row", rows, d)
        return column_block, total

    col = ("z", "core")
    in_specs = (P(None, "row", col), P(None, col, None), P(None, "row", None), P())
    out_specs = (P(None, ("row", "z", "core"), None), P())
    return jax.shard_map(
        per_device, mesh=fine, in_specs=in_specs, out_specs=out_specs, check_vma=False
    )
```

```python
import functools

import jax
import jax.numpy as jnp
from jax import lax
from jax.experimental import pallas as pl
from jax.experimental.pallas import tpu as pltpu
from jax.sharding import Mesh, PartitionSpec as P

B = 256


def multiply_tiles(deep, rows, place, *refs):
    far, slots, (out_ref, spread) = refs[:deep], refs[deep : deep + rows], refs[deep + rows :]
    groups, height, chunk = far[0].shape
    piece = slots[0].shape[2]
    for s in range(groups):
        for d in range(deep):
            slot = place[s * deep + d]
            for e in range(rows):
                first = pl.multiple_of(place[groups * deep + e] * piece, piece)
                spread[s, d, pl.ds(first, piece)] = slots[e][slot, s]
    tiles = (out_ref.shape[1] - height) // chunk
    for s in range(groups):
        wide = jnp.concatenate([piece_ref[s] for piece_ref in far], axis=1)
        tall = spread[s].reshape(deep * chunk, spread.shape[3])
        out_ref[s, :height] = jnp.dot(
            wide, tall, precision=lax.Precision.HIGHEST, preferred_element_type=jnp.float32
        )
        for t in range(tiles):
            own = spread[s, place[groups * deep + rows + t]]
            out_ref[s, height + t * chunk : height + (t + 1) * chunk] = own


def solution(mesh):
    rows, cols = mesh.shape["row"], mesh.shape["col"]
    cores, deep = 2, cols // 2
    fine = Mesh(mesh.devices.reshape(rows, deep, cores), ("row", "z", "core"))
    highest = lax.Precision.HIGHEST

    def shifted(array, axis, size, shift):
        return lax.ppermute(array, axis, [(i, (i + shift) % size) for i in range(size)])

    def traded(array, axis, size, other):
        return lax.ppermute(array, axis, [(i, i ^ other) for i in range(size)])

    def gathered(array, axis, size):
        return [array] + [traded(array, axis, size, d) for d in range(1, size)]

    def per_device(ancestor, panel, factor_inv, pattern):
        row = lax.axis_index("row")
        z = lax.axis_index("z")
        core = lax.axis_index("core")
        groups, chunk, width = panel.shape
        depth = factor_inv.shape[1]
        part = width // deep
        piece = chunk // rows
        out_rows = ancestor.shape[1] // cols
        tiles = ancestor.shape[1] // B

        def picked(slots, place, at):
            value = slots[0]
            for d in range(1, len(slots)):
                value = jnp.where(place ^ at == d, slots[d], value)
            return value

        early = [d for d in range(1, deep) if not deep < 4 * d < 3 * deep]
        late = [d for d in range(1, deep) if d not in early]
        far = {d: shifted(ancestor, "z", deep, d) for d in early[:1]}

        mine = lax.dynamic_slice_in_dim(panel, row * depth, depth, axis=2)
        partial = jnp.einsum("srw,swv->srv", mine, factor_inv, precision=highest)
        partial, held_back = lax.optimization_barrier((partial, ancestor))
        far |= {d: shifted(held_back, "z", deep, d) for d in early[1:]}

        def rows_of(r):
            return lax.dynamic_slice_in_dim(partial, r * piece, piece, axis=1)

        sums = [traded(rows_of(row ^ d), "row", rows, d) for d in range(1, rows)]
        squares = jnp.sum(lax.dynamic_slice_in_dim(factor_inv, z * part, part, axis=2) ** 2, axis=1)
        sums, squares = lax.optimization_barrier((sums, squares))
        scaled = sum(sums, rows_of(row))

        def columns_of(array, c):
            return lax.dynamic_slice_in_dim(array, c * part, part, axis=2)

        slots = [columns_of(scaled, z)]
        for d in range(1, deep):
            slots.append(traded(columns_of(scaled, z ^ d), "z", deep, d))
        if deep > 1:
            for d in late:
                far[d] = shifted(far[d - 1], "z", deep, 1)
        slots = gathered(jnp.stack(slots), "row", rows)

        count = jnp.arange(deep, dtype=jnp.int32)
        at = (z - count) % deep
        stored = jnp.sum(
            jnp.where(pattern[:, :, None] == at, count[:, None], 0), axis=1, dtype=jnp.int32
        )
        from_z = (z ^ stored).reshape(-1)
        quarter = row ^ jnp.arange(rows, dtype=jnp.int32)
        own_tile = (z - row * tiles - jnp.arange(tiles, dtype=jnp.int32)) % deep
        place = jnp.concatenate([from_z, quarter, own_tile])
        height = ancestor.shape[1]
        whole = pl.BlockSpec(memory_space=pltpu.VMEM)
        product = pl.pallas_call(
            functools.partial(multiply_tiles, deep, rows),
            out_shape=jax.ShapeDtypeStruct((groups, height + tiles * chunk, part), jnp.float32),
            in_specs=[pl.BlockSpec(memory_space=pltpu.SMEM)] + [whole] * (deep + rows),
            out_specs=whole,
            scratch_shapes=[pltpu.VMEM((groups, deep, chunk, part), jnp.float32)],
            compiler_params=pltpu.CompilerParams(vmem_limit_bytes=32 * 1024 * 1024),
        )(place, ancestor, *[far[d] for d in range(1, deep)], *slots)
        other = shifted(product, "core", cores, 1)

        own, own_other = [
            array[:, height:].reshape(groups, tiles, chunk, part) for array in (product, other)
        ]
        product = product[:, :height] + other[:, :height]
        halves = [jnp.where(core == 0, own, own_other), jnp.where(core == 0, own_other, own)]
        own = jnp.stack(halves, axis=2).reshape(groups, height, part)
        term = jnp.sum(own * product, axis=1) + squares
        tail = jnp.concatenate([term, jnp.zeros((-groups % 8, part), jnp.float32)])

        def rows_for(c):
            block = lax.dynamic_slice_in_dim(product, (c * cores + core) * out_rows, out_rows, axis=1)
            return jnp.concatenate([block.reshape(groups * out_rows, part), tail])

        moved = [rows_for(z)]
        for d in range(1, deep):
            moved.append(traded(rows_for(z ^ d), "z", deep, d))
        moved = jnp.concatenate([picked(moved, z, c) for c in range(deep)], axis=1)
        column_block = -moved[: groups * out_rows].reshape(groups, out_rows, width)
        total = moved[groups * out_rows : groups * out_rows + groups]
        local = total
        for d in range(1, rows):
            total = total + traded(local, "row", rows, d)
        return column_block, total

    col = ("z", "core")
    in_specs = (P(None, "row", col), P(None, col, None), P(None, "row", None), P())
    out_specs = (P(None, ("row", "z", "core"), None), P())
    return jax.shard_map(
        per_device, mesh=fine, in_specs=in_specs, out_specs=out_specs, check_vma=False
    )
```
